256 devices in a mesh: replica: 8 (over z_lo, core), fsdp: 32 (over z_hi, y, x).
Axes of the slice: x: 4, y: 4, z: 8 (z_hi: 2, z_lo: 4; z = z_hi * 4 + z_lo), core: 2. Of those that a mesh axis runs over, the one named last changes fastest.
Arguments:
- layer_index: int32 [8], P('replica'), may hold values from 0 to 3
- inputs: bfloat16 [65536, 4608], P(('replica', 'fsdp')), may hold values from -24 to 24
- norm_gain: float32 [4608], replicated, may hold values from 0.1 to 1.9
- cotangent: bfloat16 [65536, 1024], P(('replica', 'fsdp')), may hold values from -6 to 6
- local_fragment: bfloat16 [8, 4, 4608, 1024], P('replica', None, 'fsdp'), may hold values from -6 to 6
- global_fragment: float32 [4, 4608, 1024], P(None, 'fsdp'), may hold values from -6 to 6
- momentum: float32 [4, 4608, 1024], P(None, 'fsdp'), may hold values from -4 to 4
Outputs:
- keys_block: bfloat16 [65536, 1024], P(('replica', 'fsdp'))
- weight_grad: float32 [8, 4608, 1024], P('replica', 'fsdp')
- new_global: float32 [4, 4608, 1024], P(None, 'fsdp')
- new_momentum: float32 [4, 4608, 1024], P(None, 'fsdp')
The draws below stay inside these ranges and needn't reach their ends.
Inputs may be any that keep to these rules, and one draw needn't show every extreme that they name: `layer_index`: a layer of the fragment for each replica.
All inputs are finite; a program needn't handle non-finite values.
Results may differ from the reference program's by a relative error of at most 0.0049.
Values may be sent and summed in bfloat16 or wider, within the bound.
No kernel may reach another device: no remote copies, remote signals or barrier semaphores. Data moves between devices by JAX's collectives and lax.ppermute only.
A program may use at most 128 MiB of HBM per device.

```python
import jax
import jax.numpy as jnp
from jax import lax

D = 4608
KV = 1024
FRAG = 4
TOKENS = 8192
ALL_TOKENS = 65536
N_REPLICA = 8


def place_ends(result, rng, least, top_value):
    longest = result.shape.index(max(result.shape))
    spots = []
    for shift in (0, 1):
        where = [jax.random.randint(jax.random.fold_in(rng, axis), (), 0, length) for axis, length in enumerate(result.shape)]
        where[longest] = (where[longest] + shift) % result.shape[longest]
        spots.append(tuple(where))
    return result.at[spots[0]].set(least).at[spots[1]].set(top_value)


def strengthened(entries, own_key, source, target, parts, factor):
    def block_of(dim):
        return (jnp.arange(entries.shape[dim]) // (entries.shape[dim] // parts)).reshape((-1,) + (1,) * (entries.ndim - 1 - dim))

    first = jax.random.permutation(own_key, parts)[block_of(target)]
    far = (block_of(target) + parts // 2) % parts
    return jnp.where((block_of(source) == first) | (block_of(source) == far), factor * entries, entries)


def level_of(own_key, shape, split, smallest, top_value):
    def one(axis_at, blocks):
        draws = jax.random.uniform(jax.random.fold_in(jax.random.fold_in(own_key, 6), axis_at), (blocks,), jnp.float32, smallest / len(split), top_value / len(split))
        return jnp.repeat(jnp.exp(draws), shape[axis_at] // blocks).reshape((-1,) + (1,) * (len(shape) - axis_at - 1))

    gain = one(*split[0])
    for cut in split[1:]:
        gain = gain * one(*cut)
    return gain


def gaussian(rng, dims, spread, reach, pieces=(), dtype=jnp.bfloat16):
    result = jax.random.normal(rng, dims, jnp.float32) * spread
    if len(pieces) > 0:
        result = level_of(rng, dims, pieces, -0.22, 0.18) * result
    return jnp.clip(result, min=-reach, max=reach).astype(dtype)


def bell_draw_with(key, extent, spread, bound, cuts, heavy, held_as=jnp.bfloat16):
    values = spread * jax.random.normal(key, extent, jnp.float32)
    if cuts:
        values = values * level_of(key, extent, cuts, -0.22, 0.18)
    return jnp.clip(strengthened(values, jax.random.fold_in(key, 3), *heavy), -bound, bound).astype(held_as)


def setup_inputs(seed: int = 0) -> dict:
    keys = jax.random.split(jax.random.key(seed), 8)
    return {
        "layer_index": place_ends(jax.random.randint(keys[0], (N_REPLICA,), 0, FRAG), jax.random.fold_in(keys[0], 1), 0, FRAG - 1).astype(jnp.int32),
        "inputs": bell_draw_with(keys[1], (ALL_TOKENS, D), 1.0, 24.0, ((0, 256),), (0, 1, 256, 6.0)),
        "norm_gain": jnp.clip(1.0 + 0.18 * jax.random.normal(keys[2], (D,), jnp.float32), 0.1, 1.9),
        "cotangent": gaussian(keys[3], (ALL_TOKENS, KV), 1.0, 6.0, ((0, 256),)),
        "local_fragment": gaussian(keys[4], (N_REPLICA, FRAG, D, KV), 1.0, 6.0, ((0, 8), (2, 32))),
        "global_fragment": gaussian(keys[5], (FRAG, D, KV), 1.0, 6.0, ((1, 32),), jnp.float32),
        "momentum": gaussian(keys[6], (FRAG, D, KV), 0.5, 4.0, ((1, 32),), jnp.float32),
    }


def reference(layer_index, inputs, norm_gain, cotangent, local_fragment, global_fragment, momentum):
    scale_factor = float(D) ** (-0.5)
    token_blocks = inputs.reshape(N_REPLICA, TOKENS, D)
    cot_blocks = cotangent.reshape(N_REPLICA, TOKENS, KV)

    def one_replica(packed):
        chosen, tokens_here, cot_here, fragment_here = packed
        values = tokens_here.astype(jnp.float32)
        stats = lax.optimization_barrier(jnp.mean(values * values, axis=1, keepdims=True))
        normed = (values * lax.rsqrt(stats + 1e-06) * norm_gain[None, :]).astype(jnp.bfloat16)
        layer = lax.dynamic_index_in_dim(fragment_here, chosen.astype(jnp.int32), 0, keepdims=False)
        keys_here = (jnp.dot(normed, layer, preferred_element_type=jnp.float32) * scale_factor).astype(jnp.bfloat16)
        grad_here = jnp.dot(normed.T, cot_here, preferred_element_type=jnp.float32) * scale_factor
        return (keys_here, grad_here)
    keys_all, weight_grad = lax.map(one_replica, (layer_index, token_blocks, cot_blocks, local_fragment))
    keys_block = keys_all.reshape(ALL_TOKENS, KV)
    delta = global_fragment[None] - local_fragment.astype(jnp.float32)
    average = lax.optimization_barrier(jnp.sum(delta, axis=0)) / N_REPLICA
    new_momentum = 0.9 * momentum + average
    new_global = global_fragment - 0.7 * (average + 0.9 * new_momentum)
    return (keys_block, weight_grad, new_global, new_momentum)
```

```python
import jax
import jax.numpy as jnp
from jax import lax
from jax.experimental import pallas as pl
from jax.experimental.pallas import tpu as pltpu
from jax.sharding import PartitionSpec as P

D = 4608
KV = 1024
ROWS = 144
WIDE = 576
TOK = 256
SCALE = float(D) ** -0.5
BF = jnp.bfloat16
F32 = jnp.float32
LIMIT = 48 * 1024 * 1024


def _place():
    f = lax.axis_index("fsdp")
    r = lax.axis_index("replica")
    return r // 2, r % 2, f // 16, (f // 4) % 4, f % 4


def _shift_y(v, k):
    perm = [(i, (i // 16) * 16 + ((i // 4 + k) % 4) * 4 + i % 4) for i in range(32)]
    return lax.ppermute(v, "fsdp", perm)


def _shift_x(v, k):
    return lax.ppermute(v, "fsdp", [(i, (i // 4) * 4 + (i + k) % 4) for i in range(32)])


def _swap_zh(v):
    return lax.ppermute(v, "fsdp", [(i, (i + 16) % 32) for i in range(32)])


def _shift_zl(v, k):
    return lax.ppermute(v, "replica", [(i, (i + 2 * k) % 8) for i in range(8)])


def _swap_core(v):
    return lax.ppermute(v, "replica", [(i, i ^ 1) for i in range(8)])


def _call(kernel, name, outs, scratch=(), flops=0, traffic=0, **kw):
    return pl.pallas_call(
        kernel,
        name=name,
        out_shape=[jax.ShapeDtypeStruct(s, d) for s, d in outs],
        scratch_shapes=list(scratch),
        compiler_params=pltpu.CompilerParams(vmem_limit_bytes=LIMIT),
        cost_estimate=pl.CostEstimate(flops=flops, bytes_accessed=traffic, transcendentals=0),
        **kw,
    )


def _vmem(n):
    return [pl.BlockSpec(memory_space=pltpu.VMEM)] * n


def _pick_kernel(index_ref, frag_ref, used_ref, s1_ref, s2_ref, s3_ref, own_ref, sems):
    zl = _place()[0]
    copies = [pltpu.make_async_copy(frag_ref.at[0, index_ref[0]], used_ref, sems.at[0])]
    for k, out in ((1, s1_ref), (2, s2_ref), (3, s3_ref), (0, own_ref)):
        copies.append(pltpu.make_async_copy(frag_ref.at[0, (zl + k) % 4], out, sems.at[k + 1]))
    for c in copies:
        c.start()
    for c in copies:
        c.wait()


def _norm_kernel(x_ref, gain_ref, *rest):
    outs, held = rest[:8], rest[8]
    _, _, zh, y, _ = _place()
    values = x_ref[...].astype(F32)
    stats = jnp.mean(values * values, axis=1, keepdims=True)
    normed = (values * lax.rsqrt(stats + 1e-06) * gain_ref[...]).astype(BF)
    for q in range(8):
        held[q] = normed[:, q * WIDE : (q + 1) * WIDE]
    for h in range(2):
        half = (zh + 1 - h) % 2
        for k in range(4):
            outs[h * 4 + k][...] = held[half * 4 + (y + k) % 4]


def _grad_kernel(n0, n1, n2, n3, c0, c1, c2, c3, own_ref, o1_ref, o2_ref, o3_ref, total):
    x = _place()[4]
    normed = jnp.concatenate([n0[...], n1[...], n2[...], n3[...]], axis=0)
    cot = jnp.concatenate([c0[...], c1[...], c2[...], c3[...]], axis=0)
    total[...] = lax.dot_general(normed, cot, (((0,), (0,)), ((), ())), preferred_element_type=F32)
    for k, out in ((0, own_ref), (1, o1_ref), (2, o2_ref), (3, o3_ref)):
        first = pl.multiple_of(((x + k) % 4) * ROWS, 16)
        out[...] = (total[pl.ds(first, ROWS), :] * SCALE).astype(out.dtype)


def _keys_kernel(*refs):
    other, own = refs[0:4], refs[4:8]
    pairs = refs[8:12]
    outs = refs[12:16]
    layer = refs[16]
    x = _place()[4]
    for k in range(4):
        first = pl.multiple_of(((x + 4 - k) % 4) * ROWS, 16)
        for h in range(2):
            layer[h, pl.ds(first, ROWS), :] = pairs[k][h]
    for k in range(4):
        part = jnp.dot(other[k][...], layer[0], preferred_element_type=F32)
        part += jnp.dot(own[k][...], layer[1], preferred_element_type=F32)
        outs[k][...] = (part * SCALE).astype(outs[k].dtype)


def _outer_kernel(place_ref, own_ref, near_ref, far_ref, global_ref, momentum_ref, new_global_ref, new_momentum_ref, average):
    k = pl.program_id(0)
    core = place_ref[1]

    @pl.when(k == 0)
    def _():
        average[...] = own_ref[...].reshape(2, ROWS // 2, KV)

    @pl.when(k > 0)
    def _():
        average[core] = near_ref[k - 1]
        average[1 - core] = far_ref[k - 1]

    mean = average[...].reshape(ROWS, KV)
    shared = global_ref[0]
    momentum = 0.9 * momentum_ref[0] + mean
    new_momentum_ref[0] = momentum
    new_global_ref[0] = shared - 0.7 * (mean + 0.9 * momentum)


def body(layer_index, inputs, norm_gain, cotangent, local_fragment, global_fragment, momentum):
    zl, core, zh, y, x = _place()
    any_spec = pl.BlockSpec(memory_space=pl.ANY)

    used, s1, s2, s3, s0 = _call(
        _pick_kernel,
        "pick",
        [((ROWS, KV), BF)] * 5,
        [pltpu.SemaphoreType.DMA((5,))],
        traffic=3_000_000,
        in_specs=[pl.BlockSpec(memory_space=pltpu.SMEM), any_spec],
        out_specs=[any_spec] * 5,
    )(layer_index, local_fragment)
    used_other = _swap_zh(used)
    cot = [cotangent] + [_shift_y(cotangent, k) for k in (1, 2, 3)]

    rows = 64
    pieces = _call(
        _norm_kernel,
        "normed",
        [((TOK, WIDE), BF)] * 8,
        [pltpu.VMEM((8, rows, WIDE), BF)],
        traffic=5_000_000,
        flops=20_000_000,
        grid=(TOK // rows,),
        in_specs=[pl.BlockSpec((rows, D), lambda i: (i, 0)), pl.BlockSpec((1, D), lambda i: (0, 0))],
        out_specs=[pl.BlockSpec((rows, WIDE), lambda i: (i, 0))] * 8,
    )(inputs, norm_gain[None, :])
    other = [pieces[0]] + [_shift_y(pieces[k], k) for k in (1, 2, 3)]
    own = [pieces[4]] + [_shift_y(pieces[4 + k], k) for k in (1, 2, 3)]

    pair = jnp.stack([used_other, used])
    pairs = [pair] + [_shift_x(pair, k) for k in (1, 2, 3)]

    locals_ = [s0] + [_shift_zl(s, k) for s, k in ((s1, 1), (s2, 2), (s3, 3))]
    shared = lax.dynamic_index_in_dim(global_fragment, zl, 0, keepdims=False)
    delta = sum(shared - v.astype(F32) for v in locals_)
    average = (delta + _swap_core(delta)) / 8.0
    half = lax.dynamic_slice_in_dim(average, core * (ROWS // 2), ROWS // 2, 0)
    near = jnp.stack([_shift_zl(half, k) for k in (1, 2, 3)])
    far = _swap_core(near)

    def by_layer(k, place):
        return ((place[0] + 4 - k) % 4, 0, 0)

    block = pl.BlockSpec((1, ROWS, KV), by_layer)
    whole = lambda *shape: pl.BlockSpec(shape, lambda k, place: (0,) * len(shape))
    new_global, new_momentum = pl.pallas_call(
        _outer_kernel,
        name="outer_step",
        out_shape=[jax.ShapeDtypeStruct((4, ROWS, KV), F32)] * 2,
        grid_spec=pltpu.PrefetchScalarGridSpec(
            num_scalar_prefetch=1,
            grid=(4,),
            in_specs=[whole(ROWS, KV), whole(3, ROWS // 2, KV), whole(3, ROWS // 2, KV), block, block],
            out_specs=[block, block],
            scratch_shapes=[pltpu.VMEM((2, ROWS // 2, KV), F32)],
        ),
        compiler_params=pltpu.CompilerParams(vmem_limit_bytes=LIMIT),
        cost_estimate=pl.CostEstimate(flops=4_000_000, bytes_accessed=12_000_000, transcendentals=0),
    )(jnp.stack([zl, core]).astype(jnp.int32), average, near, far, global_fragment, momentum)

    def grad(parts):
        return _call(
            _grad_kernel,
            "grad",
            [((ROWS, KV), F32)] + [((ROWS, KV), BF)] * 3,
            [pltpu.VMEM((WIDE, KV), F32)],
            flops=2 * WIDE * KV * 4 * TOK,
            traffic=5_000_000,
            in_specs=_vmem(8),
            out_specs=_vmem(4),
        )(*parts, *cot)

    g0, g1, g2, g3 = grad(other)
    far_sum = g0 + sum(_shift_x(g, k).astype(F32) for g, k in ((g1, 1), (g2, 2), (g3, 3)))
    from_zh = _swap_zh(far_sum.astype(BF))
    g0, g1, g2, g3 = grad(own)
    near_sum = g0 + sum(_shift_x(g, k).astype(F32) for g, k in ((g1, 1), (g2, 2), (g3, 3)))
    weight_grad = (near_sum + from_zh.astype(F32))[None]

    k0, k1, k2, k3 = _call(
        _keys_kernel,
        "keys",
        [((TOK, KV), F32)] + [((TOK, KV), BF)] * 3,
        [pltpu.VMEM((2, WIDE, KV), BF)],
        flops=2 * 4 * TOK * 2 * WIDE * KV,
        traffic=8_000_000,
        in_specs=_vmem(12),
        out_specs=_vmem(4),
    )(*other, *own, *pairs)
    keys = k0 + sum(_shift_y(v, -k).astype(F32) for v, k in ((k1, 1), (k2, 2), (k3, 3)))
    return keys.astype(BF), weight_grad, new_global, new_momentum


def solution(mesh):
    placed = (
        P("replica"),
        P(("replica", "fsdp"), None),
        P(),
        P(("replica", "fsdp"), None),
        P("replica", None, "fsdp", None),
        P(None, "fsdp", None),
        P(None, "fsdp", None),
    )
    return jax.shard_map(
        body,
        mesh=mesh,
        in_specs=placed,
        out_specs=(
            P(("replica", "fsdp"), None),
            P("replica", "fsdp", None),
            P(None, "fsdp", None),
            P(None, "fsdp", None),
        ),
        check_vma=False,
    )
```

```python
import jax
import jax.numpy as jnp
from jax import lax
from jax.experimental import pallas as pl
from jax.experimental.pallas import tpu as pltpu
from jax.sharding import PartitionSpec as P

D = 4608
KV = 1024
ROWS = 144
WIDE = 576
TOK = 256
MSG = 2 * WIDE + KV
SCALE = float(D) ** -0.5
BF = jnp.bfloat16
F32 = jnp.float32
LIMIT = 48 * 1024 * 1024


def _place():
    f = lax.axis_index("fsdp")
    r = lax.axis_index("replica")
    return r >> 1, r & 1, f >> 4, (f >> 2) & 3, f & 3


def _shift_y(v, k):
    perm = [(i, (i // 16) * 16 + ((i // 4 + k) % 4) * 4 + i % 4) for i in range(32)]
    return lax.ppermute(v, "fsdp", perm)


def _shift_x(v, k):
    return lax.ppermute(v, "fsdp", [(i, (i // 4) * 4 + (i + k) % 4) for i in range(32)])


def _swap_zh(v):
    return lax.ppermute(v, "fsdp", [(i, (i + 16) % 32) for i in range(32)])


def _shift_zl(v, k):
    return lax.ppermute(v, "replica", [(i, (i + 2 * k) % 8) for i in range(8)])


def _send_far(v):
    return lax.ppermute(v, "replica", [(i, (i + 2 + 4 * (i % 2)) % 8) for i in range(8)])


def _after(v, *done):
    return lax.optimization_barrier((v, *done))[0]


def _swap_core(v):
    return lax.ppermute(v, "replica", [(i, i ^ 1) for i in range(8)])


def _call(kernel, name, outs, scratch=(), flops=0, traffic=0, **kw):
    return pl.pallas_call(
        kernel,
        name=name,
        out_shape=[jax.ShapeDtypeStruct(s, d) for s, d in outs],
        scratch_shapes=list(scratch),
        compiler_params=pltpu.CompilerParams(vmem_limit_bytes=LIMIT),
        cost_estimate=pl.CostEstimate(flops=flops, bytes_accessed=traffic, transcendentals=0),
        **kw,
    )


def _vmem(n):
    return [pl.BlockSpec(memory_space=pltpu.VMEM)] * n


def _pick_kernel(index_ref, frag_ref, used_ref, s1_ref, s2_ref, s3_ref, own_ref, sems):
    zl = _place()[0]
    copies = [pltpu.make_async_copy(frag_ref.at[0, index_ref[0]], used_ref, sems.at[0])]
    for k, out in ((1, s1_ref), (2, s2_ref), (3, s3_ref), (0, own_ref)):
        copies.append(pltpu.make_async_copy(frag_ref.at[0, (zl + k) & 3], out, sems.at[k + 1]))
    for c in copies:
        c.start()
    for c in copies:
        c.wait()


def _norm_kernel(x_ref, gain_ref, cot_ref, own_ref, m1_ref, m2_ref, m3_ref, held):
    _, _, zh, y, _ = _place()
    values = x_ref[...].astype(F32)
    stats = jnp.mean(values * values, axis=1, keepdims=True)
    normed = (values * lax.rsqrt(stats + 1e-06) * gain_ref[...]).astype(BF)
    for q in range(8):
        held[q] = normed[:, q * WIDE : (q + 1) * WIDE]
    for k, out in enumerate((own_ref, m1_ref, m2_ref, m3_ref)):
        chunk = (y + k) & 3
        out[:, : 2 * WIDE] = jnp.concatenate([held[(1 - zh) * 4 + chunk], held[zh * 4 + chunk]], axis=1)
        if k:
            out[:, 2 * WIDE :] = cot_ref[...]


def _grad_kernel(n_ref, c_ref, m1_ref, m2_ref, m3_ref, *rest):
    outs, total = rest[:8], rest[8]
    x = _place()[4]
    messages = (m1_ref, m2_ref, m3_ref)
    normed = jnp.concatenate([n_ref[...]] + [m[:, : 2 * WIDE] for m in messages], axis=0)
    cot = jnp.concatenate([c_ref[...]] + [m[:, 2 * WIDE :] for m in messages], axis=0)
    total[...] = lax.dot_general(normed, cot, (((0,), (0,)), ((), ())), preferred_element_type=F32)
    for h in range(2):
        for k in range(4):
            first = pl.multiple_of(h * WIDE + ((x + k) & 3) * ROWS, 16)
            out = outs[h * 4 + k]
            out[...] = (total[pl.ds(first, ROWS), :] * SCALE).astype(out.dtype)


def _keys_kernel(*refs):
    blocks, pairs, outs, layer = refs[0:4], refs[4:8], refs[8:12], refs[12]
    x = _place()[4]
    for k in range(4):
        for h in range(2):
            first = pl.multiple_of(h * WIDE + ((x + 4 - k) & 3) * ROWS, 16)
            layer[pl.ds(first, ROWS), :] = pairs[k][h]
    for k in range(4):
        part = jnp.dot(blocks[k][:, : 2 * WIDE], layer[...], preferred_element_type=F32)
        outs[k][...] = (part * SCALE).astype(outs[k].dtype)


def _outer_kernel(place_ref, own_ref, a_ref, b_ref, near_ref, far_ref, global_ref, momentum_ref, new_global_ref, new_momentum_ref, average):
    k = pl.program_id(0)
    core = place_ref[1]
    half = ROWS // 2

    @pl.when(k == 0)
    def _():
        average[...] = own_ref[...].reshape(2, half, KV)

    @pl.when(k == 1)
    def _():
        average[...] = a_ref[...].reshape(2, half, KV)

    @pl.when(k == 2)
    def _():
        average[...] = b_ref[...].reshape(2, half, KV)

    @pl.when(k == 3)
    def _():
        average[core] = near_ref[...]
        average[1 - core] = far_ref[...]

    mean = average[...].reshape(ROWS, KV)
    shared = global_ref[0]
    momentum = 0.9 * momentum_ref[0] + mean
    new_momentum_ref[0] = momentum
    new_global_ref[0] = shared - 0.7 * (mean + 0.9 * momentum)


def body(layer_index, inputs, norm_gain, cotangent, local_fragment, global_fragment, momentum):
    zl, core, zh, y, x = _place()
    any_spec = pl.BlockSpec(memory_space=pl.ANY)

    used, s1, s2, s3, s0 = _call(
        _pick_kernel,
        "pick",
        [((ROWS, KV), BF)] * 5,
        [pltpu.SemaphoreType.DMA((5,))],
        traffic=3_000_000,
        in_specs=[pl.BlockSpec(memory_space=pltpu.SMEM), any_spec],
        out_specs=[any_spec] * 5,
    )(layer_index, local_fragment)
    used_other = _swap_zh(used)

    rows = 64
    tile = lambda n: pl.BlockSpec((rows, n), lambda i: (i, 0))
    own, m1, m2, m3 = _call(
        _norm_kernel,
        "normed",
        [((TOK, 2 * WIDE), BF)] + [((TOK, MSG), BF)] * 3,
        [pltpu.VMEM((8, rows, WIDE), BF)],
        traffic=7_000_000,
        flops=20_000_000,
        grid=(TOK // rows,),
        in_specs=[tile(D), pl.BlockSpec((1, D), lambda i: (0, 0)), tile(KV)],
        out_specs=[tile(2 * WIDE)] + [tile(MSG)] * 3,
    )(inputs, _after(norm_gain[None, :], used), cotangent)
    r1 = _shift_y(m1, 1)
    r3 = _shift_y(m3, 3)
    r2 = _shift_y(_after(m2, r1, r3), 2)
    messages = [r1, r2, r3]

    pair = jnp.stack([used_other, used])
    p1 = _shift_x(pair, 1)
    p3 = _shift_x(pair, 3)
    p2 = _shift_x(_after(pair, p1, p3), 2)
    pairs = [pair, p1, p2, p3]

    t1 = _shift_zl(s1, 1)
    t3 = _shift_zl(s3, 3)
    t2 = _shift_zl(_after(s2, t1, t3, used_other), 2)
    shared = lax.dynamic_index_in_dim(global_fragment, zl, 0, keepdims=False)
    delta = sum(shared - v.astype(F32) for v in (s0, t1, t2, t3))
    average = (delta + _swap_core(_after(delta, p1, p3))) / 8.0
    half = lax.dynamic_slice_in_dim(average, core * (ROWS // 2), ROWS // 2, 0)
    sent = _send_far(average)
    near = _shift_zl(half, 2)
    swapped = _swap_core(sent)
    far = _swap_core(near)

    def by_layer(k, place):
        step = jnp.where(k == 1, 3 - 2 * place[1], jnp.where(k == 2, 1 + 2 * place[1], jnp.where(k == 3, 2, 0)))
        return ((place[0] + step) & 3, 0, 0)

    block = pl.BlockSpec((1, ROWS, KV), by_layer)
    whole = lambda *shape: pl.BlockSpec(shape, lambda k, place: (0,) * len(shape))
    new_global, new_momentum = pl.pallas_call(
        _outer_kernel,
        name="outer_step",
        out_shape=[jax.ShapeDtypeStruct((4, ROWS, KV), F32)] * 2,
        grid_spec=pltpu.PrefetchScalarGridSpec(
            num_scalar_prefetch=1,
            grid=(4,),
            in_specs=[whole(ROWS, KV)] * 3 + [whole(ROWS // 2, KV)] * 2 + [block, block],
            out_specs=[block, block],
            scratch_shapes=[pltpu.VMEM((2, ROWS // 2, KV), F32)],
        ),
        compiler_params=pltpu.CompilerParams(vmem_limit_bytes=LIMIT),
        cost_estimate=pl.CostEstimate(flops=4_000_000, bytes_accessed=12_000_000, transcendentals=0),
    )(jnp.stack([zl, core]).astype(jnp.int32), average, sent, swapped, near, far, global_fragment, momentum)

    g = _call(
        _grad_kernel,
        "grad",
        ([((ROWS, KV), F32)] + [((ROWS, KV), BF)] * 3) * 2,
        [pltpu.VMEM((2 * WIDE, KV), F32)],
        flops=2 * 2 * WIDE * KV * 4 * TOK,
        traffic=8_000_000,
        in_specs=_vmem(5),
        out_specs=_vmem(8),
    )(own, cotangent, *messages)
    a = [_shift_x(g[k], k) for k in (1, 3, 2)]
    far_sum = g[0] + sum(v.astype(F32) for v in a)
    from_zh = _swap_zh(far_sum.astype(BF))
    b = [_shift_x(_after(g[4 + k], a[2]), k) for k in (1, 3, 2)]
    weight_grad = (g[4] + sum(v.astype(F32) for v in b) + from_zh.astype(F32))[None]

    k0, k1, k2, k3 = _call(
        _keys_kernel,
        "keys",
        [((TOK, KV), F32)] + [((TOK, KV), BF)] * 3,
        [pltpu.VMEM((2 * WIDE, KV), BF)],
        flops=2 * 4 * TOK * 2 * WIDE * KV,
        traffic=8_000_000,
        in_specs=_vmem(8),
        out_specs=_vmem(4),
    )(own, *messages, *pairs)
    e1 = _shift_y(k1, 3)
    e3 = _shift_y(k3, 1)
    e2 = _shift_y(_after(k2, e1, e3), 2)
    keys = k0 + sum(v.astype(F32) for v in (e1, e3, e2))
    return keys.astype(BF), weight_grad, new_global, new_momentum


def solution(mesh):
    placed = (
        P("replica"),
        P(("replica", "fsdp"), None),
        P(),
        P(("replica", "fsdp"), None),
        P("replica", None, "fsdp", None),
        P(None, "fsdp", None),
        P(None, "fsdp", None),
    )
    return jax.shard_map(
        body,
        mesh=mesh,
        in_specs=placed,
        out_specs=(
            P(("replica", "fsdp"), None),
            P("replica", "fsdp", None),
            P(None, "fsdp", None),
            P(None, "fsdp", None),
        ),
        check_vma=False,
    )
```

```python
import jax
import jax.numpy as jnp
from jax import lax
from jax.experimental import pallas as pl
from jax.experimental.pallas import tpu as pltpu
from jax.sharding import Mesh, PartitionSpec as P

D = 4608
KV = 1024
ROWS = 144
WIDE = 576
TOK = 256
MSG = 2 * WIDE + KV
SCALE = float(D) ** -0.5
BF = jnp.bfloat16
F32 = jnp.float32
LIMIT = 48 * 1024 * 1024


def _place():
    return [lax.axis_index(n) for n in ("zl", "core", "zh", "y", "x")]


def _shift(v, axis, k, size=4):
    return lax.ppermute(v, axis, [(i, (i + k) % size) for i in range(size)])


def _after(v, *done):
    return lax.optimization_barrier((v, *done))[0]


def _call(kernel, name, outs, scratch=(), flops=0, traffic=0, **kw):
    return pl.pallas_call(
        kernel,
        name=name,
        out_shape=[jax.ShapeDtypeStruct(s, d) for s, d in outs],
        scratch_shapes=list(scratch),
        compiler_params=pltpu.CompilerParams(vmem_limit_bytes=LIMIT),
        cost_estimate=pl.CostEstimate(flops=flops, bytes_accessed=traffic, transcendentals=0),
        **kw,
    )


def _vmem(n):
    return [pl.BlockSpec(memory_space=pltpu.VMEM)] * n


def _pick_kernel(index_ref, frag_ref, used_ref, give_ref, keep_ref, sems):
    core = _place()[1]
    copies = [
        pltpu.make_async_copy(frag_ref.at[0, index_ref[0]], used_ref, sems.at[0]),
        pltpu.make_async_copy(frag_ref.at[0, pl.ds(2 - 2 * core, 2)], give_ref, sems.at[1]),
        pltpu.make_async_copy(frag_ref.at[0, pl.ds(2 * core, 2)], keep_ref, sems.at[2]),
    ]
    for c in copies:
        c.start()
    for c in copies:
        c.wait()


def _norm_kernel(x_ref, gain_ref, cot_ref, own_ref, m1_ref, m2_ref, m3_ref, held):
    _, _, zh, y, _ = _place()
    values = x_ref[...].astype(F32)
    stats = jnp.mean(values * values, axis=1, keepdims=True)
    normed = (values * lax.rsqrt(stats + 1e-06) * gain_ref[...]).astype(BF)
    for q in range(8):
        held[q] = normed[:, q * WIDE : (q + 1) * WIDE]
    for k, out in enumerate((own_ref, m1_ref, m2_ref, m3_ref)):
        chunk = (y + k) & 3
        out[:, : 2 * WIDE] = jnp.concatenate([held[(1 - zh) * 4 + chunk], held[zh * 4 + chunk]], axis=1)
        if k:
            out[:, 2 * WIDE :] = cot_ref[...]


def _grad_kernel(n_ref, c_ref, m1_ref, m2_ref, m3_ref, *rest):
    outs, total = rest[:8], rest[8]
    x = _place()[4]
    messages = (m1_ref, m2_ref, m3_ref)
    normed = jnp.concatenate([n_ref[...]] + [m[:, : 2 * WIDE] for m in messages], axis=0)
    cot = jnp.concatenate([c_ref[...]] + [m[:, 2 * WIDE :] for m in messages], axis=0)
    total[...] = lax.dot_general(normed, cot, (((0,), (0,)), ((), ())), preferred_element_type=F32)
    for h in range(2):
        for k in range(4):
            first = pl.multiple_of(h * WIDE + ((x + k) & 3) * ROWS, 16)
            out = outs[h * 4 + k]
            out[...] = (total[pl.ds(first, ROWS), :] * SCALE).astype(out.dtype)


def _keys_kernel(*refs):
    blocks, pairs, outs, layer = refs[0:4], refs[4:8], refs[8:12], refs[12]
    x = _place()[4]
    for k in range(4):
        for h in range(2):
            first = pl.multiple_of(h * WIDE + ((x + 4 - k) & 3) * ROWS, 16)
            layer[pl.ds(first, ROWS), :] = pairs[k][h]
    for k in range(4):
        part = jnp.dot(blocks[k][:, : 2 * WIDE], layer[...], preferred_element_type=F32)
        outs[k][...] = (part * SCALE).astype(outs[k].dtype)


def _outer_kernel(core_ref, own_ref, far_ref, global_ref, momentum_ref, new_global_ref, new_momentum_ref):
    k = pl.program_id(0)

    def write(mean):
        momentum = 0.9 * momentum_ref[0] + mean
        new_momentum_ref[0] = momentum
        new_global_ref[0] = global_ref[0] - 0.7 * (mean + 0.9 * momentum)

    @pl.when(k < 2)
    def _():
        write(own_ref[k])

    @pl.when(k >= 2)
    def _():
        write(far_ref[k - 2])


def body(layer_index, inputs, norm_gain, cotangent, local_fragment, global_fragment, momentum):
    core = lax.axis_index("core")
    any_spec = pl.BlockSpec(memory_space=pl.ANY)

    used, give, keep = _call(
        _pick_kernel,
        "pick",
        [((ROWS, KV), BF)] + [((2, ROWS, KV), BF)] * 2,
        [pltpu.SemaphoreType.DMA((3,))],
        traffic=3_000_000,
        in_specs=[pl.BlockSpec(memory_space=pltpu.SMEM), any_spec],
        out_specs=[any_spec] * 3,
    )(layer_index, local_fragment)
    used_other = _shift(used, "zh", 1, 2)
    got = _shift(give, "core", 1, 2)

    rows = 64
    tile = lambda n: pl.BlockSpec((rows, n), lambda i: (i, 0))
    own, m1, m2, m3 = _call(
        _norm_kernel,
        "normed",
        [((TOK, 2 * WIDE), BF)] + [((TOK, MSG), BF)] * 3,
        [pltpu.VMEM((8, rows, WIDE), BF)],
        traffic=7_000_000,
        flops=20_000_000,
        grid=(TOK // rows,),
        in_specs=[tile(D), pl.BlockSpec((1, D), lambda i: (0, 0)), tile(KV)],
        out_specs=[tile(2 * WIDE)] + [tile(MSG)] * 3,
    )(inputs, _after(norm_gain[None, :], used), cotangent)
    shared = lax.dynamic_slice_in_dim(global_fragment, 2 * core, 2, 0)
    delta = (shared - keep.astype(F32)) + (shared - _after(got, own).astype(F32))
    summed = lax.psum_scatter(delta.reshape(2 * ROWS, KV), "zl", tiled=True)
    r1, r3 = _shift(m1, "y", 1), _shift(m3, "y", 3)
    messages = [r1, _shift(_after(m2, r1, r3, used_other, summed), "y", 2), r3]

    pair = jnp.stack([_after(used_other, r1, r3), used])
    pairs = [pair] + [_shift(pair, "x", k) for k in (1, 2, 3)]

    g = _call(
        _grad_kernel,
        "grad",
        ([((ROWS, KV), F32)] + [((ROWS, KV), BF)] * 3) * 2,
        [pltpu.VMEM((2 * WIDE, KV), F32)],
        flops=2 * 2 * WIDE * KV * 4 * TOK,
        traffic=8_000_000,
        in_specs=_vmem(5),
        out_specs=_vmem(8),
    )(own, cotangent, *messages)
    a = [_shift(g[k], "x", k) for k in (1, 3, 2)]
    far_sum = g[0] + sum(v.astype(F32) for v in a)
    from_zh = _shift(far_sum.astype(BF), "zh", 1, 2)
    b = [_shift(_after(g[4 + k], a[2]), "x", k) for k in (1, 3, 2)]
    weight_grad = (g[4] + sum(v.astype(F32) for v in b) + from_zh.astype(F32))[None]

    k0, k1, k2, k3 = _call(
        _keys_kernel,
        "keys",
        [((TOK, KV), F32)] + [((TOK, KV), BF)] * 3,
        [pltpu.VMEM((2 * WIDE, KV), BF)],
        flops=2 * 4 * TOK * 2 * WIDE * KV,
        traffic=8_000_000,
        in_specs=_vmem(8),
        out_specs=_vmem(4),
    )(own, *messages, *pairs)
    average = _after(lax.all_gather(summed / 8.0, "zl", tiled=True).reshape(2, ROWS, KV), k0)
    far = _shift(average, "core", 1, 2)

    def by_layer(k, place):
        return ((k + 2 * place[0]) & 3, 0, 0)

    block = pl.BlockSpec((1, ROWS, KV), by_layer)
    whole = pl.BlockSpec((2, ROWS, KV), lambda k, place: (0, 0, 0))
    new_global, new_momentum = pl.pallas_call(
        _outer_kernel,
        name="outer_step",
        out_shape=[jax.ShapeDtypeStruct((4, ROWS, KV), F32)] * 2,
        grid_spec=pltpu.PrefetchScalarGridSpec(
            num_scalar_prefetch=1,
            grid=(4,),
            in_specs=[whole, whole, block, block],
            out_specs=[block, block],
        ),
        compiler_params=pltpu.CompilerParams(vmem_limit_bytes=LIMIT),
        cost_estimate=pl.CostEstimate(flops=4_000_000, bytes_accessed=12_000_000, transcendentals=0),
    )(core.astype(jnp.int32)[None], average, far, global_fragment, momentum)

    e1 = _shift(k1, "y", 3)
    e3 = _shift(k3, "y", 1)
    e2 = _shift(_after(k2, e1, e3), "y", 2)
    keys = k0 + sum(v.astype(F32) for v in (e1, e3, e2))
    return keys.astype(BF), weight_grad, new_global, new_momentum


def solution(mesh):
    split = Mesh(mesh.devices.reshape(4, 2, 2, 4, 4), ("zl", "core", "zh", "y", "x"))
    replica, fsdp = ("zl", "core"), ("zh", "y", "x")
    placed = (
        P(replica),
        P(replica + fsdp, None),
        P(),
        P(replica + fsdp, None),
        P(replica, None, fsdp, None),
        P(None, fsdp, None),
        P(None, fsdp, None),
    )
    return jax.shard_map(
        body,
        mesh=split,
        in_specs=placed,
        out_specs=(
            P(replica + fsdp, None),
            P(replica, fsdp, None),
            P(None, fsdp, None),
            P(None, fsdp, None),
        ),
        check_vma=False,
    )
```

```python
import jax
import jax.numpy as jnp
from jax import lax
from jax.experimental import pallas as pl
from jax.experimental.pallas import tpu as pltpu
from jax.sharding import Mesh, PartitionSpec as P

D = 4608
KV = 1024
ROWS = 144
WIDE = 576
TOK = 256
MSG = 2 * WIDE + KV
SCALE = float(D) ** -0.5
BF = jnp.bfloat16
F32 = jnp.float32
F16 = jnp.float16
UNIT = 512.0
LIMIT = 48 * 1024 * 1024


def _place():
    return [lax.axis_index(n) for n in ("zl", "core", "zh", "y", "x")]


def _shift(v, axis, k, size=4):
    return lax.ppermute(v, axis, [(i, (i + k) % size) for i in range(size)])


def _flip(v, axis, bit, size=4):
    return lax.ppermute(v, axis, [(i, i ^ bit) for i in range(size)])


def _after(v, *done):
    return lax.optimization_barrier((v, *done))[0]


def _call(kernel, name, outs, scratch=(), flops=0, traffic=0, **kw):
    return pl.pallas_call(
        kernel,
        name=name,
        out_shape=[jax.ShapeDtypeStruct(s, d) for s, d in outs],
        scratch_shapes=list(scratch),
        compiler_params=pltpu.CompilerParams(vmem_limit_bytes=LIMIT),
        cost_estimate=pl.CostEstimate(flops=0, bytes_accessed=1024, transcendentals=0),
        **kw,
    )


def _vmem(n):
    return [pl.BlockSpec(memory_space=pltpu.VMEM)] * n


def _pick_kernel(index_ref, frag_ref, used_ref, give_ref, keep_ref, sems):
    core = _place()[1]
    copies = [
        pltpu.make_async_copy(frag_ref.at[0, index_ref[0]], used_ref, sems.at[0]),
        pltpu.make_async_copy(frag_ref.at[0, pl.ds(2 - 2 * core, 2)], give_ref, sems.at[1]),
        pltpu.make_async_copy(frag_ref.at[0, pl.ds(2 * core, 2)], keep_ref, sems.at[2]),
    ]
    for c in copies:
        c.start()
    for c in copies:
        c.wait()


def _norm_kernel(x_ref, gain_ref, cot_ref, own_ref, m1_ref, m2_ref, m3_ref, held):
    _, _, zh, y, _ = _place()
    values = x_ref[...].astype(F32)
    stats = jnp.mean(values * values, axis=1, keepdims=True)
    normed = (values * lax.rsqrt(stats + 1e-06) * gain_ref[...]).astype(BF)
    for q in range(8):
        held[q] = normed[:, q * WIDE : (q + 1) * WIDE]
    for k, out in enumerate((own_ref, m1_ref, m2_ref, m3_ref)):
        chunk = (y + k) & 3
        out[:, : 2 * WIDE] = jnp.concatenate([held[(1 - zh) * 4 + chunk], held[zh * 4 + chunk]], axis=1)
        if k:
            out[:, 2 * WIDE :] = cot_ref[...]


def _grad_kernel(n_ref, c_ref, m1_ref, m2_ref, m3_ref, *rest):
    outs, total = rest[:8], rest[8]
    x = _place()[4]
    messages = (m1_ref, m2_ref, m3_ref)
    normed = jnp.concatenate([n_ref[...]] + [m[:, : 2 * WIDE] for m in messages], axis=0)
    cot = jnp.concatenate([c_ref[...]] + [m[:, 2 * WIDE :] for m in messages], axis=0)
    total[...] = lax.dot_general(normed, cot, (((0,), (0,)), ((), ())), preferred_element_type=F32)
    for h in range(2):
        for k in range(4):
            first = pl.multiple_of(h * WIDE + ((x + k) & 3) * ROWS, 16)
            out = outs[h * 4 + k]
            out[...] = (total[pl.ds(first, ROWS), :] * SCALE).astype(out.dtype)


def _keys_kernel(*refs):
    blocks, pairs, outs, layer = refs[0:4], refs[4:8], refs[8:12], refs[12]
    x = _place()[4]
    for k in range(4):
        for h in range(2):
            first = pl.multiple_of(h * WIDE + ((x + 4 - k) & 3) * ROWS, 16)
            layer[pl.ds(first, ROWS), :] = pairs[k][h]
    for k in range(4):
        part = jnp.dot(blocks[k][:, : 2 * WIDE], layer[...], preferred_element_type=F32)
        outs[k][...] = (part * SCALE).astype(outs[k].dtype)


def _outer_kernel(place_ref, *refs):
    averages, (global_ref, momentum_ref, new_global_ref, new_momentum_ref) = refs[:4], refs[4:]

    for k in range(4):

        @pl.when(pl.program_id(0) == k)
        def _():
            mean = averages[k][...]
            momentum = 0.9 * momentum_ref[0] + mean
            new_momentum_ref[0] = momentum
            new_global_ref[0] = global_ref[0] - 0.7 * (mean + 0.9 * momentum)


def body(layer_index, inputs, norm_gain, cotangent, local_fragment, global_fragment, momentum):
    zl, core = lax.axis_index("zl"), lax.axis_index("core")
    hi, lo = zl >> 1, zl & 1
    any_spec = pl.BlockSpec(memory_space=pl.ANY)

    used, give, keep = _call(
        _pick_kernel,
        "pick",
        [((ROWS, KV), BF)] + [((2, ROWS, KV), BF)] * 2,
        [pltpu.SemaphoreType.DMA((3,))],
        traffic=3_000_000,
        in_specs=[pl.BlockSpec(memory_space=pltpu.SMEM), any_spec],
        out_specs=[any_spec] * 3,
    )(layer_index, local_fragment)
    used_other = _shift(used, "zh", 1, 2)
    got = _shift(give, "core", 1, 2)

    rows = 64
    tile = lambda n: pl.BlockSpec((rows, n), lambda i: (i, 0))
    own, m1, m2, m3 = _call(
        _norm_kernel,
        "normed",
        [((TOK, 2 * WIDE), BF)] + [((TOK, MSG), BF)] * 3,
        [pltpu.VMEM((8, rows, WIDE), BF)],
        traffic=7_000_000,
        flops=20_000_000,
        grid=(TOK // rows,),
        in_specs=[tile(D), pl.BlockSpec((1, D), lambda i: (0, 0)), tile(KV)],
        out_specs=[tile(2 * WIDE)] + [tile(MSG)] * 3,
    )(inputs, _after(norm_gain[None, :], used), cotangent)
    got = _after(got, own)

    def delta(which):
        shared = lax.dynamic_index_in_dim(global_fragment, 2 * core + which, 0, keepdims=False)
        first = lax.dynamic_index_in_dim(keep, which, 0, keepdims=False).astype(F32)
        second = lax.dynamic_index_in_dim(got, which, 0, keepdims=False).astype(F32)
        return ((shared - first) + (shared - second)) * UNIT

    half = ROWS // 2
    sum4 = delta(hi) + _flip(delta(1 - hi).astype(F16), "zl", 2).astype(F32)
    out = lax.dynamic_slice_in_dim(sum4, (1 - lo) * half, half, 0).astype(F16)
    sum8 = lax.dynamic_slice_in_dim(sum4, lo * half, half, 0) + _flip(out, "zl", 1).astype(F32)

    r1, r3 = _shift(m1, "y", 1), _shift(m3, "y", 3)
    messages = [r1, _shift(_after(m2, r1, r3, sum4), "y", 2), r3]

    pair = jnp.stack([used_other, used])
    p1, p3 = _shift(pair, "x", 1), _shift(pair, "x", 3)
    pairs = [pair, p1, _shift(_after(pair, p1, p3), "x", 2), p3]

    sum8 = sum8.astype(F16)
    peer = _flip(sum8, "zl", 1)
    mine = jnp.where(lo == 0, jnp.concatenate([sum8, peer]), jnp.concatenate([peer, sum8]))
    next_layer = _flip(mine, "zl", 2)
    averages = [mine, next_layer, _shift(mine, "core", 1, 2), _shift(next_layer, "core", 1, 2)]
    averages = [v.astype(F32) / (8.0 * UNIT) for v in averages]

    def layer_of(k, place):
        return (jnp.where(k < 2, place[0], 1 - place[0]) * 2 + (place[1] ^ (k & 1)), 0, 0)

    block = pl.BlockSpec((1, ROWS, KV), layer_of)
    whole = pl.BlockSpec((ROWS, KV), lambda k, place: (0, 0))
    new_global, new_momentum = pl.pallas_call(
        _outer_kernel,
        name="outer_step",
        out_shape=[jax.ShapeDtypeStruct((4, ROWS, KV), F32)] * 2,
        grid_spec=pltpu.PrefetchScalarGridSpec(
            num_scalar_prefetch=1,
            grid=(4,),
            in_specs=[whole] * 4 + [block, block],
            out_specs=[block, block],
        ),
        compiler_params=pltpu.CompilerParams(vmem_limit_bytes=LIMIT),
        cost_estimate=pl.CostEstimate(flops=0, bytes_accessed=1024, transcendentals=0),
    )(jnp.stack([core, hi]).astype(jnp.int32), *averages, global_fragment, momentum)

    g = _call(
        _grad_kernel,
        "grad",
        ([((ROWS, KV), F32)] + [((ROWS, KV), BF)] * 3) * 2,
        [pltpu.VMEM((2 * WIDE, KV), F32)],
        flops=2 * 2 * WIDE * KV * 4 * TOK,
        traffic=8_000_000,
        in_specs=_vmem(5),
        out_specs=_vmem(8),
    )(own, cotangent, *messages)
    a = [_shift(g[k], "x", k) for k in (1, 3, 2)]
    far_sum = g[0] + sum(v.astype(F32) for v in a)
    from_zh = _shift(far_sum.astype(BF), "zh", 1, 2)
    b = [_shift(_after(g[4 + k], a[2]), "x", k) for k in (1, 3, 2)]
    weight_grad = (g[4] + sum(v.astype(F32) for v in b) + from_zh.astype(F32))[None]

    k0, k1, k2, k3 = _call(
        _keys_kernel,
        "keys",
        [((TOK, KV), F32)] + [((TOK, KV), BF)] * 3,
        [pltpu.VMEM((2 * WIDE, KV), BF)],
        flops=2 * 4 * TOK * 2 * WIDE * KV,
        traffic=8_000_000,
        in_specs=_vmem(8),
        out_specs=_vmem(4),
    )(_after(own, next_layer), *messages, *pairs)
    e1 = _shift(k1, "y", 3)
    e3 = _shift(k3, "y", 1)
    e2 = _shift(_after(k2, e1, e3), "y", 2)
    keys = k0 + sum(v.astype(F32) for v in (e1, e3, e2))
    return keys.astype(BF), weight_grad, new_global, new_momentum


def solution(mesh):
    split = Mesh(mesh.devices.reshape(4, 2, 2, 4, 4), ("zl", "core", "zh", "y", "x"))
    replica, fsdp = ("zl", "core"), ("zh", "y", "x")
    placed = (
        P(replica),
        P(replica + fsdp, None),
        P(),
        P(replica + fsdp, None),
        P(replica, None, fsdp, None),
        P(None, fsdp, None),
        P(None, fsdp, None),
    )
    return jax.shard_map(
        body,
        mesh=split,
        in_specs=placed,
        out_specs=(
            P(replica + fsdp, None),
            P(replica, fsdp, None),
            P(None, fsdp, None),
            P(None, fsdp, None),
        ),
        check_vma=False,
    )
```

```python
import functools

import jax
import jax.numpy as jnp
from jax import lax
from jax.experimental import pallas as pl
from jax.experimental.pallas import tpu as pltpu
from jax.sharding import Mesh, PartitionSpec as P

D = 4608
KV = 1024
ROWS = 144
WIDE = 576
TOK = 256
MSG = 2 * WIDE + KV
SCALE = float(D) ** -0.5
BF = jnp.bfloat16
F32 = jnp.float32
F16 = jnp.float16
UNIT = 512.0
LIMIT = 48 * 1024 * 1024


def _place():
    return [lax.axis_index(n) for n in ("zl", "core", "zh", "y", "x")]


def _shift(v, axis, k, size=4):
    return lax.ppermute(v, axis, [(i, (i + k) % size) for i in range(size)])


def _flip(v, axis, bit, size=4):
    return lax.ppermute(v, axis, [(i, i ^ bit) for i in range(size)])


def _after(v, *done):
    return lax.optimization_barrier((v, *done))[0]


def _call(kernel, name, outs, scratch=(), **kw):
    return pl.pallas_call(
        kernel,
        name=name,
        out_shape=[jax.ShapeDtypeStruct(s, d) for s, d in outs],
        scratch_shapes=list(scratch),
        compiler_params=pltpu.CompilerParams(vmem_limit_bytes=LIMIT),
        cost_estimate=pl.CostEstimate(flops=0, bytes_accessed=1024, transcendentals=0),
        **kw,
    )


def _vmem(n):
    return [pl.BlockSpec(memory_space=pltpu.VMEM)] * n


def _pick_kernel(index_ref, frag_ref, used_ref, give_ref, keep_ref, sems):
    core = _place()[1]
    copies = [
        pltpu.make_async_copy(frag_ref.at[0, index_ref[0]], used_ref, sems.at[0]),
        pltpu.make_async_copy(frag_ref.at[0, pl.ds(2 - 2 * core, 2)], give_ref, sems.at[1]),
        pltpu.make_async_copy(frag_ref.at[0, pl.ds(2 * core, 2)], keep_ref, sems.at[2]),
    ]
    for c in copies:
        c.start()
    for c in copies:
        c.wait()


def _norm_kernel(x_ref, gain_ref, cot_ref, own_ref, n1_ref, m2_ref, n3_ref, held):
    _, _, zh, y, _ = _place()
    values = x_ref[...].astype(F32)
    stats = jnp.mean(values * values, axis=1, keepdims=True)
    normed = (values * lax.rsqrt(stats + 1e-06) * gain_ref[...]).astype(BF)
    for q in range(8):
        held[q] = normed[:, q * WIDE : (q + 1) * WIDE]
    for k, out in enumerate((own_ref, n1_ref, m2_ref, n3_ref)):
        chunk = (y + k) & 3
        out[:, : 2 * WIDE] = jnp.concatenate([held[(1 - zh) * 4 + chunk], held[zh * 4 + chunk]], axis=1)
    m2_ref[:, 2 * WIDE :] = cot_ref[...]


def _grad_kernel(half, n0, c0, n1, c1, m2, n3, c3, own_ref, o1_ref, o2_ref, o3_ref, total):
    x = _place()[4]
    first = half * WIDE
    normed = jnp.concatenate([n[:, first : first + WIDE] for n in (n0, n1, m2, n3)], axis=0)
    cot = jnp.concatenate([c0[...], c1[...], m2[:, 2 * WIDE :], c3[...]], axis=0)
    total[...] = lax.dot_general(normed, cot, (((0,), (0,)), ((), ())), preferred_element_type=F32)
    for k, out in enumerate((own_ref, o1_ref, o2_ref, o3_ref)):
        rows = pl.ds(pl.multiple_of(((x + k) & 3) * ROWS, 16), ROWS)
        out[...] = (total[rows, :] * SCALE).astype(out.dtype)


def _keys_kernel(n, *refs):
    blocks, pairs, outs, layer = refs[:n], refs[n : n + 4], refs[n + 4 : 2 * n + 4], refs[-1]
    x = _place()[4]
    for k in range(4):
        for h in range(2):
            first = pl.multiple_of(h * WIDE + ((x + 4 - k) & 3) * ROWS, 16)
            layer[pl.ds(first, ROWS), :] = pairs[k][h]
    for block, out in zip(blocks, outs):
        part = jnp.dot(block[:, : 2 * WIDE], layer[...], preferred_element_type=F32)
        out[...] = (part * SCALE).astype(out.dtype)


def _outer_kernel(place_ref, *refs):
    averages, (global_ref, momentum_ref, new_global_ref, new_momentum_ref) = refs[:4], refs[4:]

    for k in range(4):

        @pl.when(pl.program_id(0) == k)
        def _():
            mean = averages[k][...]
            momentum = 0.9 * momentum_ref[0] + mean
            new_momentum_ref[0] = momentum
            new_global_ref[0] = global_ref[0] - 0.7 * (mean + 0.9 * momentum)


def body(layer_index, inputs, norm_gain, cotangent, local_fragment, global_fragment, momentum):
    zl, core = lax.axis_index("zl"), lax.axis_index("core")
    hi, lo = zl >> 1, zl & 1
    any_spec = pl.BlockSpec(memory_space=pl.ANY)

    used, give, keep = _call(
        _pick_kernel,
        "pick",
        [((ROWS, KV), BF)] + [((2, ROWS, KV), BF)] * 2,
        [pltpu.SemaphoreType.DMA((3,))],
        in_specs=[pl.BlockSpec(memory_space=pltpu.SMEM), any_spec],
        out_specs=[any_spec] * 3,
    )(layer_index, local_fragment)
    c1, c3 = _shift(cotangent, "y", 1), _shift(cotangent, "y", 3)
    used_other = _shift(used, "zh", 1, 2)
    got = _shift(give, "core", 1, 2)

    rows = 64
    tile = lambda n: pl.BlockSpec((rows, n), lambda i: (i, 0))
    own, n1, m2, n3 = _call(
        _norm_kernel,
        "normed",
        [((TOK, n), BF) for n in (2 * WIDE, 2 * WIDE, MSG, 2 * WIDE)],
        [pltpu.VMEM((8, rows, WIDE), BF)],
        grid=(TOK // rows,),
        in_specs=[tile(D), pl.BlockSpec((1, D), lambda i: (0, 0)), tile(KV)],
        out_specs=[tile(n) for n in (2 * WIDE, 2 * WIDE, MSG, 2 * WIDE)],
    )(inputs, _after(norm_gain[None, :], used), cotangent)

    pair = jnp.stack([used_other, used])
    p1, p3 = _shift(pair, "x", 1), _shift(pair, "x", 3)
    r1, r3 = _shift(_after(n1, c1, c3), "y", 1), _shift(_after(n3, c1, c3), "y", 3)

    got = _after(got, own, used_other)

    def delta(which):
        shared = lax.dynamic_index_in_dim(global_fragment, 2 * core + which, 0, keepdims=False)
        first = lax.dynamic_index_in_dim(keep, which, 0, keepdims=False).astype(F32)
        second = lax.dynamic_index_in_dim(got, which, 0, keepdims=False).astype(F32)
        return ((shared - first) + (shared - second)) * UNIT

    half = ROWS // 2
    sum4 = delta(lo) + _after(_flip(delta(1 - lo).astype(F16), "zl", 1), r1, r3).astype(F32)
    out = lax.dynamic_slice_in_dim(sum4, (1 - hi) * half, half, 0).astype(F16)
    other = _after(_flip(out, "zl", 2), p1, p3)
    sum8 = (lax.dynamic_slice_in_dim(sum4, hi * half, half, 0) + other.astype(F32)).astype(F16)
    peer = _flip(sum8, "zl", 2)
    mine = jnp.where(hi == 0, jnp.concatenate([sum8, peer]), jnp.concatenate([peer, sum8]))
    next_layer = _flip(mine, "zl", 1)

    r2 = _shift(_after(m2, r1, r3, pair), "y", 2)
    pairs = [pair, p1, _shift(_after(pair, r1, r3), "x", 2), p3]

    def keys_of(*blocks):
        return _call(
            functools.partial(_keys_kernel, len(blocks)),
            f"keys{len(blocks)}",
            [((TOK, KV), F32 if b is own else BF) for b in blocks],
            [pltpu.VMEM((2 * WIDE, KV), BF)],
            in_specs=_vmem(len(blocks) + 4),
            out_specs=_vmem(len(blocks)),
        )(*blocks, *pairs)

    k0, k1, k3 = keys_of(own, _after(r1, mine), r3)
    e1, e3 = _shift(k1, "y", 3), _shift(k3, "y", 1)

    def grad(half, own):
        return _call(
            functools.partial(_grad_kernel, half),
            f"grad{half}",
            [((ROWS, KV), F32)] + [((ROWS, KV), BF)] * 3,
            [pltpu.VMEM((WIDE, KV), F32)],
            in_specs=_vmem(7),
            out_specs=_vmem(4),
        )(own, cotangent, r1, c1, r2, r3, c3)

    g = grad(0, _after(own, k0))
    a1, a3 = _shift(g[1], "x", 1), _shift(g[3], "x", 3)
    b = grad(1, own)
    (k2,) = keys_of(_after(r2, g[0]))
    a2 = _shift(_after(g[2], a1, b[0], k2), "x", 2)
    far_sum = (g[0] + sum(v.astype(F32) for v in (a1, a2, a3))).astype(BF)
    from_zh = _shift(far_sum, "zh", 1, 2)
    near_sum = _after(b[0] + from_zh.astype(F32))
    b1, b3, b2 = [_shift(_after(b[k], far_sum), "x", k) for k in (1, 3, 2)]
    weight_grad = (near_sum + sum(v.astype(F32) for v in (b1, b3, b2)))[None]

    averages = [mine, next_layer] + [_shift(_after(v, a1, a3), "core", 1, 2) for v in (mine, next_layer)]
    averages = [v.astype(F32) / (8.0 * UNIT) for v in averages]

    def layer_of(k, place):
        return (jnp.where(k < 2, place[0], 1 - place[0]) * 2 + (place[1] ^ (k & 1)), 0, 0)

    block = pl.BlockSpec((1, ROWS, KV), layer_of)
    whole = pl.BlockSpec((ROWS, KV), lambda k, place: (0, 0))
    new_global, new_momentum = pl.pallas_call(
        _outer_kernel,
        name="outer_step",
        out_shape=[jax.ShapeDtypeStruct((4, ROWS, KV), F32)] * 2,
        grid_spec=pltpu.PrefetchScalarGridSpec(
            num_scalar_prefetch=1,
            grid=(4,),
            in_specs=[whole] * 4 + [block, block],
            out_specs=[block, block],
        ),
        compiler_params=pltpu.CompilerParams(vmem_limit_bytes=LIMIT),
        cost_estimate=pl.CostEstimate(flops=0, bytes_accessed=1024, transcendentals=0),
    )(jnp.stack([core, lo]).astype(jnp.int32), *averages, global_fragment, momentum)

    e2 = _shift(_after(k2, e1, e3, b[0], a1, a3, next_layer), "y", 2)
    keys = k0 + sum(v.astype(F32) for v in (e1, e3, e2))
    return keys.astype(BF), weight_grad, new_global, new_momentum


def solution(mesh):
    split = Mesh(mesh.devices.reshape(4, 2, 2, 4, 4), ("zl", "core", "zh", "y", "x"))
    replica, fsdp = ("zl", "core"), ("zh", "y", "x")
    placed = (
        P(replica),
        P(replica + fsdp, None),
        P(),
        P(replica + fsdp, None),
        P(replica, None, fsdp, None),
        P(None, fsdp, None),
        P(None, fsdp, None),
    )
    return jax.shard_map(
        body,
        mesh=split,
        in_specs=placed,
        out_specs=(
            P(replica + fsdp, None),
            P(replica, fsdp, None),
            P(None, fsdp, None),
            P(None, fsdp, None),
        ),
        check_vma=False,
    )
```

```python
import functools

import jax
import jax.numpy as jnp
from jax import lax
from jax.experimental import pallas as pl
from jax.experimental.pallas import tpu as pltpu
from jax.sharding import Mesh, PartitionSpec as P

D = 4608
KV = 1024
ROWS = 144
WIDE = 576
TOK = 256
MSG = 2 * WIDE + KV
SCALE = float(D) ** -0.5
BF = jnp.bfloat16
F32 = jnp.float32
F16 = jnp.float16
UNIT = 512.0
LIMIT = 48 * 1024 * 1024


def _place():
    return [lax.axis_index(n) for n in ("zl", "core", "zh", "y", "x")]


def _shift(v, axis, k, size=4):
    return lax.ppermute(v, axis, [(i, (i + k) % size) for i in range(size)])


def _flip(v, axis, bit, size=4):
    return lax.ppermute(v, axis, [(i, i ^ bit) for i in range(size)])


def _after(v, *done):
    return lax.optimization_barrier((v, *done))[0]


def _call(kernel, name, outs, scratch=(), **kw):
    return pl.pallas_call(
        kernel,
        name=name,
        out_shape=[jax.ShapeDtypeStruct(s, d) for s, d in outs],
        scratch_shapes=list(scratch),
        compiler_params=pltpu.CompilerParams(vmem_limit_bytes=LIMIT),
        cost_estimate=pl.CostEstimate(flops=0, bytes_accessed=1024, transcendentals=0),
        **kw,
    )


def _vmem(n):
    return [pl.BlockSpec(memory_space=pltpu.VMEM)] * n


def _pick_kernel(index_ref, frag_ref, used_ref, give_ref, keep_ref, sems):
    core = _place()[1]
    copies = [
        pltpu.make_async_copy(frag_ref.at[0, index_ref[0]], used_ref, sems.at[0]),
        pltpu.make_async_copy(frag_ref.at[0, pl.ds(2 - 2 * core, 2)], give_ref, sems.at[1]),
        pltpu.make_async_copy(frag_ref.at[0, pl.ds(2 * core, 2)], keep_ref, sems.at[2]),
    ]
    for c in copies:
        c.start()
    for c in copies:
        c.wait()


def _norm_kernel(x_ref, gain_ref, cot_ref, own_ref, n1_ref, m2_ref, n3_ref, held):
    _, _, zh, y, _ = _place()
    values = x_ref[...].astype(F32)
    stats = jnp.mean(values * values, axis=1, keepdims=True)
    normed = (values * lax.rsqrt(stats + 1e-06) * gain_ref[...]).astype(BF)
    for q in range(8):
        held[q] = normed[:, q * WIDE : (q + 1) * WIDE]
    for k, out in enumerate((own_ref, n1_ref, m2_ref, n3_ref)):
        chunk = (y + k) & 3
        out[:, : 2 * WIDE] = jnp.concatenate([held[(1 - zh) * 4 + chunk], held[zh * 4 + chunk]], axis=1)
    m2_ref[:, 2 * WIDE :] = cot_ref[...]


def _grad_kernel(half, n0, c0, n1, c1, m2, n3, c3, own_ref, o1_ref, o2_ref, o3_ref, total):
    x = _place()[4]
    first = half * WIDE
    normed = jnp.concatenate([n[:, first : first + WIDE] for n in (n0, n1, m2, n3)], axis=0)
    cot = jnp.concatenate([c0[...], c1[...], m2[:, 2 * WIDE :], c3[...]], axis=0)
    total[...] = lax.dot_general(normed, cot, (((0,), (0,)), ((), ())), preferred_element_type=F32)
    for k, out in enumerate((own_ref, o1_ref, o2_ref, o3_ref)):
        rows = pl.ds(pl.multiple_of(((x + k) & 3) * ROWS, 16), ROWS)
        out[...] = (total[rows, :] * SCALE).astype(out.dtype)


def _keys_kernel(n, *refs):
    blocks, pairs, outs, layer = refs[:n], refs[n : n + 4], refs[n + 4 : 2 * n + 4], refs[-1]
    x = _place()[4]
    for k in range(4):
        for h in range(2):
            first = pl.multiple_of(h * WIDE + ((x + 4 - k) & 3) * ROWS, 16)
            layer[pl.ds(first, ROWS), :] = pairs[k][h]
    for block, out in zip(blocks, outs):
        part = jnp.dot(block[:, : 2 * WIDE], layer[...], preferred_element_type=F32)
        out[...] = (part * SCALE).astype(out.dtype)


def _outer_kernel(place_ref, *refs):
    averages, (global_ref, momentum_ref, new_global_ref, new_momentum_ref) = refs[:4], refs[4:]

    for k in range(4):

        @pl.when(pl.program_id(0) == k)
        def _():
            mean = averages[k][...]
            momentum = 0.9 * momentum_ref[0] + mean
            new_momentum_ref[0] = momentum
            new_global_ref[0] = global_ref[0] - 0.7 * (mean + 0.9 * momentum)


def body(layer_index, inputs, norm_gain, cotangent, local_fragment, global_fragment, momentum):
    zl, core = lax.axis_index("zl"), lax.axis_index("core")
    hi, lo = zl >> 1, zl & 1
    any_spec = pl.BlockSpec(memory_space=pl.ANY)

    used, give, keep = _call(
        _pick_kernel,
        "pick",
        [((ROWS, KV), BF)] + [((2, ROWS, KV), BF)] * 2,
        [pltpu.SemaphoreType.DMA((3,))],
        in_specs=[pl.BlockSpec(memory_space=pltpu.SMEM), any_spec],
        out_specs=[any_spec] * 3,
    )(layer_index, local_fragment)
    c1, c3 = _shift(cotangent, "y", 1), _shift(cotangent, "y", 3)
    used_other = _shift(used, "zh", 1, 2)
    got = _shift(give, "core", 1, 2)

    rows = 64
    tile = lambda n: pl.BlockSpec((rows, n), lambda i: (i, 0))
    own, n1, m2, n3 = _call(
        _norm_kernel,
        "normed",
        [((TOK, n), BF) for n in (2 * WIDE, 2 * WIDE, MSG, 2 * WIDE)],
        [pltpu.VMEM((8, rows, WIDE), BF)],
        grid=(TOK // rows,),
        in_specs=[tile(D), pl.BlockSpec((1, D), lambda i: (0, 0)), tile(KV)],
        out_specs=[tile(n) for n in (2 * WIDE, 2 * WIDE, MSG, 2 * WIDE)],
    )(inputs, _after(norm_gain[None, :], used), cotangent)

    pair = jnp.stack([_after(used_other, c1, c3), used])
    p1, p3 = _shift(pair, "x", 1), _shift(pair, "x", 3)
    r1, r3 = _shift(_after(n1, c1, c3), "y", 1), _shift(_after(n3, c1, c3), "y", 3)

    got = _after(got, own, used_other)

    def delta(which):
        shared = lax.dynamic_index_in_dim(global_fragment, 2 * core + which, 0, keepdims=False)
        first = lax.dynamic_index_in_dim(keep, which, 0, keepdims=False).astype(F32)
        second = lax.dynamic_index_in_dim(got, which, 0, keepdims=False).astype(F32)
        return ((shared - first) + (shared - second)) * UNIT

    half = ROWS // 2
    sum4 = delta(lo) + _after(_flip(delta(1 - lo).astype(F16), "zl", 1), r1, r3, p1, p3).astype(F32)
    out = lax.dynamic_slice_in_dim(sum4, (1 - hi) * half, half, 0).astype(F16)
    other = _flip(out, "zl", 2)
    sum8 = (lax.dynamic_slice_in_dim(sum4, hi * half, half, 0) + other.astype(F32)).astype(F16)
    peer = _flip(sum8, "zl", 2)
    mine = jnp.where(hi == 0, jnp.concatenate([sum8, peer]), jnp.concatenate([peer, sum8]))
    next_layer = _flip(mine, "zl", 1)

    r2 = _shift(_after(m2, r1, r3, pair), "y", 2)
    pairs = [pair, p1, _shift(_after(pair, p1, p3), "x", 2), p3]

    def keys_of(*blocks):
        return _call(
            functools.partial(_keys_kernel, len(blocks)),
            f"keys{len(blocks)}",
            [((TOK, KV), F32 if b is own else BF) for b in blocks],
            [pltpu.VMEM((2 * WIDE, KV), BF)],
            in_specs=_vmem(len(blocks) + 4),
            out_specs=_vmem(len(blocks)),
        )(*blocks, *pairs)

    k0, k1, k3 = keys_of(own, _after(r1, mine), r3)
    e1, e3 = _shift(k1, "y", 3), _shift(k3, "y", 1)

    def grad(half, own):
        return _call(
            functools.partial(_grad_kernel, half),
            f"grad{half}",
            [((ROWS, KV), F32)] + [((ROWS, KV), BF)] * 3,
            [pltpu.VMEM((WIDE, KV), F32)],
            in_specs=_vmem(7),
            out_specs=_vmem(4),
        )(own, cotangent, r1, c1, r2, r3, c3)

    g = grad(0, _after(own, k0))
    a1, a3 = _shift(g[1], "x", 1), _shift(g[3], "x", 3)
    b = grad(1, own)
    (k2,) = keys_of(_after(r2, b[0], e1, e3, a1, a3))
    a2 = _shift(_after(g[2], a1), "x", 2)
    swapped = [_shift(_after(v, a1, a3), "core", 1, 2) for v in (mine, next_layer)]
    far_sum = (_after(g[0], *swapped) + sum(v.astype(F32) for v in (a1, a2, a3))).astype(BF)
    from_zh = _shift(far_sum, "zh", 1, 2)
    near_sum = _after(b[0] + from_zh.astype(F32))
    b1, b3, b2 = [_shift(_after(b[k], far_sum), "x", k) for k in (1, 3, 2)]
    weight_grad = (near_sum + sum(v.astype(F32) for v in (b1, b3, b2)))[None]

    averages = [mine, next_layer] + swapped
    averages = [v.astype(F32) / (8.0 * UNIT) for v in averages]

    def layer_of(k, place):
        return (jnp.where(k < 2, place[0], 1 - place[0]) * 2 + (place[1] ^ (k & 1)), 0, 0)

    block = pl.BlockSpec((1, ROWS, KV), layer_of)
    whole = pl.BlockSpec((ROWS, KV), lambda k, place: (0, 0))
    new_global, new_momentum = pl.pallas_call(
        _outer_kernel,
        name="outer_step",
        out_shape=[jax.ShapeDtypeStruct((4, ROWS, KV), F32)] * 2,
        grid_spec=pltpu.PrefetchScalarGridSpec(
            num_scalar_prefetch=1,
            grid=(4,),
            in_specs=[whole] * 4 + [block, block],
            out_specs=[block, block],
        ),
        compiler_params=pltpu.CompilerParams(vmem_limit_bytes=LIMIT),
        cost_estimate=pl.CostEstimate(flops=0, bytes_accessed=1024, transcendentals=0),
    )(jnp.stack([core, lo]).astype(jnp.int32), *averages, global_fragment, momentum)

    e2 = _shift(_after(k2, b[0]), "y", 2)
    keys = k0 + sum(v.astype(F32) for v in (e1, e3, e2))
    return keys.astype(BF), weight_grad, new_global, new_momentum


def solution(mesh):
    split = Mesh(mesh.devices.reshape(4, 2, 2, 4, 4), ("zl", "core", "zh", "y", "x"))
    replica, fsdp = ("zl", "core"), ("zh", "y", "x")
    placed = (
        P(replica),
        P(replica + fsdp, None),
        P(),
        P(replica + fsdp, None),
        P(replica, None, fsdp, None),
        P(None, fsdp, None),
        P(None, fsdp, None),
    )
    return jax.shard_map(
        body,
        mesh=split,
        in_specs=placed,
        out_specs=(
            P(replica + fsdp, None),
            P(replica, fsdp, None),
            P(None, fsdp, None),
            P(None, fsdp, None),
        ),
        check_vma=False,
    )
```

```python
import functools

import jax
import jax.numpy as jnp
from jax import lax
from jax.experimental import pallas as pl
from jax.experimental.pallas import tpu as pltpu
from jax.sharding import Mesh, PartitionSpec as P

D = 4608
KV = 1024
ROWS = 144
WIDE = 576
TOK = 256
EARLY = 640
MSG = EARLY + KV
SCALE = float(D) ** -0.5
BF = jnp.bfloat16
F32 = jnp.float32
F16 = jnp.float16
UNIT = 512.0
LIMIT = 48 * 1024 * 1024


def _place():
    return [lax.axis_index(n) for n in ("zl", "core", "zh", "y", "x")]


def _shift(v, axis, k, size=4):
    return lax.ppermute(v, axis, [(i, (i + k) % size) for i in range(size)])


def _flip(v, axis, bit, size=4):
    return lax.ppermute(v, axis, [(i, i ^ bit) for i in range(size)])


def _after(v, *done):
    return lax.optimization_barrier((v, *done))[0]


def _call(kernel, name, outs, scratch=(), traffic=1024, **kw):
    return pl.pallas_call(
        kernel,
        name=name,
        out_shape=[jax.ShapeDtypeStruct(s, d) for s, d in outs],
        scratch_shapes=list(scratch),
        compiler_params=pltpu.CompilerParams(vmem_limit_bytes=LIMIT),
        cost_estimate=pl.CostEstimate(flops=0, bytes_accessed=traffic, transcendentals=0),
        **kw,
    )


def _vmem(n):
    return [pl.BlockSpec(memory_space=pltpu.VMEM)] * n


def _pick_kernel(index_ref, frag_ref, used_ref, give_ref, keep_ref, sems):
    core = _place()[1]
    copies = [
        pltpu.make_async_copy(frag_ref.at[0, index_ref[0]], used_ref, sems.at[0]),
        pltpu.make_async_copy(frag_ref.at[0, pl.ds(2 - 2 * core, 2)], give_ref, sems.at[1]),
        pltpu.make_async_copy(frag_ref.at[0, pl.ds(2 * core, 2)], keep_ref, sems.at[2]),
    ]
    for c in copies:
        c.start()
    for c in copies:
        c.wait()


def _pair_kernel(a_ref, b_ref, out_ref, sems):
    copies = [pltpu.make_async_copy(ref, out_ref.at[k], sems.at[k]) for k, ref in enumerate((a_ref, b_ref))]
    for c in copies:
        c.start()
    for c in copies:
        c.wait()


def _norm_kernel(x_ref, gain_ref, cot_ref, own_ref, n1_ref, n3_ref, first_ref, second_ref, held):
    _, _, zh, y, _ = _place()
    values = x_ref[...].astype(F32)
    stats = jnp.mean(values * values, axis=1, keepdims=True)
    normed = (values * lax.rsqrt(stats + 1e-06) * gain_ref[...]).astype(BF)
    for q in range(8):
        held[q] = normed[:, q * WIDE : (q + 1) * WIDE]
    other, same = (1 - zh) * 4, zh * 4
    for k, out in ((0, own_ref), (1, n1_ref), (3, n3_ref)):
        chunk = (y + k) & 3
        out[...] = jnp.concatenate([held[other + chunk], held[same + chunk]], axis=1)
    chunk = jnp.concatenate([held[other + (y ^ 2)], held[same + (y ^ 2)]], axis=1)
    first_ref[:, :EARLY] = chunk[:, :EARLY]
    first_ref[:, EARLY:] = cot_ref[...]
    second_ref[...] = chunk[:, EARLY:]


def _grad_kernel(half, n0, c0, n1, c1, n3, c3, *refs):
    far, outs, total = refs[: half + 1], refs[half + 1 : half + 5], refs[half + 5]
    x = _place()[4]
    near = slice(half * WIDE, (half + 1) * WIDE)
    n2 = far[0][:, :EARLY]
    if half:
        n2 = jnp.concatenate([n2, far[1][...]], axis=1)
    normed = jnp.concatenate([n[:, near] for n in (n0, n1, n2, n3)], axis=0)
    cot = jnp.concatenate([c0[...], c1[...], far[0][:, EARLY:], c3[...]], axis=0)
    total[...] = lax.dot_general(normed, cot, (((0,), (0,)), ((), ())), preferred_element_type=F32)
    for k, out in enumerate(outs):
        rows = pl.ds(pl.multiple_of(((x + k) & 3) * ROWS, 16), ROWS)
        out[...] = (total[rows, :] * SCALE).astype(out.dtype)


def _place_layer(pairs, layer):
    x = _place()[4]
    for k in range(4):
        for h in range(2):
            first = pl.multiple_of(h * WIDE + ((x + 4 - k) & 3) * ROWS, 16)
            layer[pl.ds(first, ROWS), :] = pairs[k][h]


def _near_keys_kernel(n0, n1, n3, p0, p1, p2, p3, o0, o1, o3, layer):
    _place_layer((p0, p1, p2, p3), layer)
    for block, out in ((n0, o0), (n1, o1), (n3, o3)):
        part = jnp.dot(block[...], layer[...], preferred_element_type=F32)
        out[...] = (part * SCALE).astype(out.dtype)


def _far_keys_kernel(first, second, p0, p1, p2, p3, out, layer):
    _place_layer((p0, p1, p2, p3), layer)
    part = jnp.dot(first[:, :EARLY], layer[:EARLY, :], preferred_element_type=F32)
    part += jnp.dot(second[...], layer[EARLY:, :], preferred_element_type=F32)
    out[...] = (part * SCALE).astype(out.dtype)


def _outer_kernel(place_ref, *refs):
    averages, (global_ref, momentum_ref, new_global_ref, new_momentum_ref) = refs[:4], refs[4:]

    for k in range(4):

        @pl.when(pl.program_id(0) == k)
        def _():
            mean = averages[k][...]
            momentum = 0.9 * momentum_ref[0] + mean
            new_momentum_ref[0] = momentum
            new_global_ref[0] = global_ref[0] - 0.7 * (mean + 0.9 * momentum)


def body(layer_index, inputs, norm_gain, cotangent, local_fragment, global_fragment, momentum):
    zl, core = lax.axis_index("zl"), lax.axis_index("core")
    hi, lo = zl >> 1, zl & 1
    any_spec = pl.BlockSpec(memory_space=pl.ANY)

    used, give, keep = _call(
        _pick_kernel,
        "pick",
        [((ROWS, KV), BF)] + [((2, ROWS, KV), BF)] * 2,
        [pltpu.SemaphoreType.DMA((3,))],
        in_specs=[pl.BlockSpec(memory_space=pltpu.SMEM), any_spec],
        out_specs=[any_spec] * 3,
    )(layer_index, local_fragment)
    c1, c3 = _shift(cotangent, "y", 1), _shift(cotangent, "y", 3)
    used_other = _shift(used, "zh", 1, 2)
    got = _shift(give, "core", 1, 2)

    rows = 64
    tile = lambda n: pl.BlockSpec((rows, n), lambda i: (i, 0))
    widths = (2 * WIDE, 2 * WIDE, 2 * WIDE, MSG, 2 * WIDE - EARLY)
    own, n1, n3, first, second = _call(
        _norm_kernel,
        "normed",
        [((TOK, n), BF) for n in widths],
        [pltpu.VMEM((8, rows, WIDE), BF)],
        grid=(TOK // rows,),
        in_specs=[tile(D), pl.BlockSpec((D,), lambda i: (0,)), tile(KV)],
        out_specs=[tile(n) for n in widths],
    )(inputs, _after(norm_gain, used), cotangent)
    r1, r3 = _shift(_after(n1, c1, c3), "y", 1), _shift(_after(n3, c1, c3), "y", 3)

    (pair,) = _call(
        _pair_kernel,
        "pair",
        [((2, ROWS, KV), BF)],
        [pltpu.SemaphoreType.DMA((2,))],
        in_specs=[any_spec] * 2,
        out_specs=[any_spec],
    )(_after(used_other, c1, c3), used)
    p1, p3 = _shift(pair, "x", 1), _shift(pair, "x", 3)
    p2 = _shift(_after(pair, r1, r3), "x", 2)
    pairs = [pair, p1, p2, p3]

    r2 = _shift(first, "y", 2)
    r4 = _shift(_after(second, r1, r3), "y", 2)

    got = _after(got, own)

    def delta(which):
        shared = lax.dynamic_index_in_dim(global_fragment, 2 * core + which, 0, keepdims=False)
        ours = lax.dynamic_index_in_dim(keep, which, 0, keepdims=False).astype(F32)
        theirs = lax.dynamic_index_in_dim(got, which, 0, keepdims=False).astype(F32)
        return ((shared - ours) + (shared - theirs)) * UNIT

    half = ROWS // 2
    near = _flip(delta(1 - lo).astype(F16), "zl", 1)
    sum4 = delta(lo) + _after(near, p1, p3).astype(F32)
    out = lax.dynamic_slice_in_dim(sum4, (1 - hi) * half, half, 0).astype(F16)
    far = _flip(_after(out, p1, p3), "zl", 2)
    sum8 = (lax.dynamic_slice_in_dim(sum4, hi * half, half, 0) + far.astype(F32)).astype(F16)
    peer = _flip(sum8, "zl", 2)
    mine = jnp.where(hi == 0, jnp.concatenate([sum8, peer]), jnp.concatenate([peer, sum8]))

    def grad(half, own, *far):
        return _call(
            functools.partial(_grad_kernel, half),
            f"grad{half}",
            [((ROWS, KV), F32)] + [((ROWS, KV), BF)] * 3,
            [pltpu.VMEM((WIDE, KV), F32)],
            in_specs=_vmem(6 + len(far)),
            out_specs=_vmem(4),
        )(own, cotangent, r1, c1, r3, c3, *far)

    def near_keys(own):
        return _call(
            _near_keys_kernel,
            "near_keys",
            [((TOK, KV), F32)] + [((TOK, KV), BF)] * 2,
            [pltpu.VMEM((2 * WIDE, KV), BF)],
            in_specs=_vmem(7),
            out_specs=_vmem(3),
        )(own, r1, r3, *pairs)

    g = grad(0, _after(own, p2), r2)
    a1, a3 = _shift(g[1], "x", 1), _shift(g[3], "x", 3)
    k0, k1, k3 = near_keys(_after(own, g[0], peer))
    e1, e3 = _shift(k1, "y", 3), _shift(k3, "y", 1)
    a2 = _shift(g[2], "x", 2)
    b = grad(1, _after(own, a1, a3), r2, r4)
    (k2,) = _call(
        _far_keys_kernel,
        "far_keys",
        [((TOK, KV), BF)],
        [pltpu.VMEM((2 * WIDE, KV), BF)],
        in_specs=_vmem(6),
        out_specs=_vmem(1),
    )(r2, _after(r4, k0), *pairs)
    next_layer = _flip(_after(mine, g[0]), "zl", 1)
    swapped = [_shift(_after(v, a1, a3), "core", 1, 2) for v in (mine, next_layer)]
    far_sum = (_after(g[0], b[0]) + sum(v.astype(F32) for v in (a1, a2, a3))).astype(BF)
    from_zh = _shift(far_sum, "zh", 1, 2)
    b1, b3 = [_shift(_after(b[k], a1, a3), "x", k) for k in (1, 3)]
    b2 = _shift(_after(b[2], far_sum, swapped[1]), "x", 2)
    weight_grad = (b[0] + sum(v.astype(F32) for v in (b1, b3, b2, from_zh)))[None]

    e2 = _shift(_after(k2, e1, e3), "y", 2)
    keys = k0 + sum(v.astype(F32) for v in (e1, e3, e2))

    averages = [mine, next_layer] + swapped
    averages = [v.astype(F32) / (8.0 * UNIT) for v in averages]

    def layer_of(k, place):
        return (jnp.where(k < 2, place[0], 1 - place[0]) * 2 + (place[1] ^ (k & 1)), 0, 0)

    block = pl.BlockSpec((1, ROWS, KV), layer_of)
    whole = pl.BlockSpec((ROWS, KV), lambda k, place: (0, 0))
    new_global, new_momentum = pl.pallas_call(
        _outer_kernel,
        name="outer_step",
        out_shape=[jax.ShapeDtypeStruct((4, ROWS, KV), F32)] * 2,
        grid_spec=pltpu.PrefetchScalarGridSpec(
            num_scalar_prefetch=1,
            grid=(4,),
            in_specs=[whole] * 4 + [block, block],
            out_specs=[block, block],
        ),
        compiler_params=pltpu.CompilerParams(vmem_limit_bytes=LIMIT),
        cost_estimate=pl.CostEstimate(flops=0, bytes_accessed=1024, transcendentals=0),
    )(jnp.stack([core, lo]).astype(jnp.int32), *averages, global_fragment, momentum)
    return keys.astype(BF), weight_grad, new_global, new_momentum


def solution(mesh):
    split = Mesh(mesh.devices.reshape(4, 2, 2, 4, 4), ("zl", "core", "zh", "y", "x"))
    replica, fsdp = ("zl", "core"), ("zh", "y", "x")
    placed = (
        P(replica),
        P(replica + fsdp, None),
        P(),
        P(replica + fsdp, None),
        P(replica, None, fsdp, None),
        P(None, fsdp, None),
        P(None, fsdp, None),
    )
    return jax.shard_map(
        body,
        mesh=split,
        in_specs=placed,
        out_specs=(
            P(replica + fsdp, None),
            P(replica, fsdp, None),
            P(None, fsdp, None),
            P(None, fsdp, None),
        ),
        check_vma=False,
    )
```

```python
import functools

import jax
import jax.numpy as jnp
from jax import lax
from jax.experimental import pallas as pl
from jax.experimental.pallas import tpu as pltpu
from jax.sharding import Mesh, PartitionSpec as P

D = 4608
KV = 1024
ROWS = 144
WIDE = 576
TOK = 256
EARLY = 640
MSG = EARLY + KV
SCALE = float(D) ** -0.5
BF = jnp.bfloat16
F32 = jnp.float32
F16 = jnp.float16
UNIT = 512.0
LIMIT = 62 * 1024 * 1024


def _place():
    return [lax.axis_index(n) for n in ("zl", "core", "zh", "y", "x")]


def _shift(v, axis, k, size=4):
    return lax.ppermute(v, axis, [(i, (i + k) % size) for i in range(size)])


def _flip(v, axis, bit, size=4):
    return lax.ppermute(v, axis, [(i, i ^ bit) for i in range(size)])


def _after(v, *done):
    return lax.optimization_barrier((v, *done))[0]


def _call(kernel, name, outs, scratch=(), traffic=1024, **kw):
    return pl.pallas_call(
        kernel,
        name=name,
        out_shape=[jax.ShapeDtypeStruct(s, d) for s, d in outs],
        scratch_shapes=list(scratch),
        compiler_params=pltpu.CompilerParams(vmem_limit_bytes=LIMIT),
        cost_estimate=pl.CostEstimate(flops=0, bytes_accessed=traffic, transcendentals=0),
        **kw,
    )


def _vmem(n):
    return [pl.BlockSpec(memory_space=pltpu.VMEM)] * n


def _pick_kernel(index_ref, frag_ref, used_ref, give_ref, keep_ref, sems):
    core = _place()[1]
    copies = [
        pltpu.make_async_copy(frag_ref.at[0, index_ref[0]], used_ref, sems.at[0]),
        pltpu.make_async_copy(frag_ref.at[0, pl.ds(2 - 2 * core, 2)], give_ref, sems.at[1]),
        pltpu.make_async_copy(frag_ref.at[0, pl.ds(2 * core, 2)], keep_ref, sems.at[2]),
    ]
    for c in copies:
        c.start()
    for c in copies:
        c.wait()


def _pair_kernel(a_ref, b_ref, out_ref, sems):
    copies = [pltpu.make_async_copy(ref, out_ref.at[k], sems.at[k]) for k, ref in enumerate((a_ref, b_ref))]
    for c in copies:
        c.start()
    for c in copies:
        c.wait()


def _norm_kernel(x_ref, gain_ref, cot_ref, own_ref, n1_ref, n3_ref, first_ref, second_ref, held):
    _, _, zh, y, _ = _place()
    values = x_ref[...].astype(F32)
    stats = jnp.mean(values * values, axis=1, keepdims=True)
    normed = (values * lax.rsqrt(stats + 1e-06) * gain_ref[...]).astype(BF)
    for q in range(8):
        held[q] = normed[:, q * WIDE : (q + 1) * WIDE]
    other, same = (1 - zh) * 4, zh * 4
    for k, out in ((0, own_ref), (1, n1_ref), (3, n3_ref)):
        chunk = (y + k) & 3
        out[...] = jnp.concatenate([held[other + chunk], held[same + chunk]], axis=1)
    chunk = jnp.concatenate([held[other + (y ^ 2)], held[same + (y ^ 2)]], axis=1)
    first_ref[:, :EARLY] = chunk[:, :EARLY]
    first_ref[:, EARLY:] = cot_ref[...]
    second_ref[...] = chunk[:, EARLY:]


def _grad_kernel(half, n0, c0, n1, c1, n3, c3, *refs):
    far, outs, total = refs[: half + 1], refs[half + 1 : half + 5], refs[half + 5]
    x = _place()[4]
    near = slice(half * WIDE, (half + 1) * WIDE)
    n2 = far[0][:, :EARLY]
    if half:
        n2 = jnp.concatenate([n2, far[1][...]], axis=1)
    normed = jnp.concatenate([n[:, near] for n in (n0, n1, n2, n3)], axis=0)
    cot = jnp.concatenate([c0[...], c1[...], far[0][:, EARLY:], c3[...]], axis=0)
    total[...] = lax.dot_general(normed, cot, (((0,), (0,)), ((), ())), preferred_element_type=F32)
    for k, out in enumerate(outs):
        rows = pl.ds(pl.multiple_of(((x + k) & 3) * ROWS, 16), ROWS)
        out[...] = (total[rows, :] * SCALE).astype(out.dtype)


def _place_layer(pairs, layer):
    x = _place()[4]
    for k in range(4):
        for h in range(2):
            first = pl.multiple_of(h * WIDE + ((x + 4 - k) & 3) * ROWS, 16)
            layer[pl.ds(first, ROWS), :] = pairs[k][h]


def _near_keys_kernel(n0, n1, n3, p0, p1, p2, p3, o0, o1, o3, layer):
    _place_layer((p0, p1, p2, p3), layer)
    for block, out in ((n0, o0), (n1, o1), (n3, o3)):
        part = jnp.dot(block[...], layer[...], preferred_element_type=F32)
        out[...] = (part * SCALE).astype(out.dtype)


def _far_keys_kernel(first, second, p0, p1, p2, p3, out, layer):
    _place_layer((p0, p1, p2, p3), layer)
    part = jnp.dot(first[:, :EARLY], layer[:EARLY, :], preferred_element_type=F32)
    part += jnp.dot(second[...], layer[EARLY:, :], preferred_element_type=F32)
    out[...] = (part * SCALE).astype(out.dtype)


def _outer_kernel(place_ref, *refs):
    averages, (global_ref, momentum_ref, new_global_ref, new_momentum_ref) = refs[:4], refs[4:]

    for k in range(4):

        @pl.when(pl.program_id(0) == k)
        def _():
            mean = averages[k][...]
            momentum = 0.9 * momentum_ref[0] + mean
            new_momentum_ref[0] = momentum
            new_global_ref[0] = global_ref[0] - 0.7 * (mean + 0.9 * momentum)


def body(layer_index, inputs, norm_gain, cotangent, local_fragment, global_fragment, momentum):
    zl, core = lax.axis_index("zl"), lax.axis_index("core")
    hi, lo = zl >> 1, zl & 1
    any_spec = pl.BlockSpec(memory_space=pl.ANY)

    used, give, keep = _call(
        _pick_kernel,
        "pick",
        [((ROWS, KV), BF)] + [((2, ROWS, KV), BF)] * 2,
        [pltpu.SemaphoreType.DMA((3,))],
        in_specs=[pl.BlockSpec(memory_space=pltpu.SMEM), any_spec],
        out_specs=[any_spec] * 3,
    )(layer_index, local_fragment)
    c1, c3 = _shift(cotangent, "y", 1), _shift(cotangent, "y", 3)
    used_other = _shift(used, "zh", 1, 2)
    got = _shift(give, "core", 1, 2)

    rows = 64
    tile = lambda n: pl.BlockSpec((rows, n), lambda i: (i, 0))
    widths = (2 * WIDE, 2 * WIDE, 2 * WIDE, MSG, 2 * WIDE - EARLY)
    own, n1, n3, first, second = _call(
        _norm_kernel,
        "normed",
        [((TOK, n), BF) for n in widths],
        [pltpu.VMEM((8, rows, WIDE), BF)],
        grid=(TOK // rows,),
        in_specs=[tile(D), pl.BlockSpec((D,), lambda i: (0,)), tile(KV)],
        out_specs=[tile(n) for n in widths],
    )(inputs, _after(norm_gain, used), cotangent)
    r1, r3 = _shift(_after(n1, c1, c3), "y", 1), _shift(_after(n3, c1, c3), "y", 3)

    (pair,) = _call(
        _pair_kernel,
        "pair",
        [((2, ROWS, KV), BF)],
        [pltpu.SemaphoreType.DMA((2,))],
        in_specs=[any_spec] * 2,
        out_specs=[any_spec],
    )(_after(used_other, c1, c3), used)
    p1, p3 = _shift(pair, "x", 1), _shift(pair, "x", 3)
    p2 = _shift(_after(pair, r1, r3), "x", 2)
    pairs = [pair, p1, p2, p3]

    r2 = _shift(first, "y", 2)
    r4 = _shift(_after(second, r1, r3), "y", 2)

    got = _after(got, own)

    def delta(which):
        shared = lax.dynamic_index_in_dim(global_fragment, 2 * core + which, 0, keepdims=False)
        ours = lax.dynamic_index_in_dim(keep, which, 0, keepdims=False).astype(F32)
        theirs = lax.dynamic_index_in_dim(got, which, 0, keepdims=False).astype(F32)
        return ((shared - ours) + (shared - theirs)) * UNIT

    half = ROWS // 2
    near = _flip(delta(1 - lo).astype(F16), "zl", 1)
    sum4 = delta(lo) + _after(near, p1, p3).astype(F32)
    out = lax.dynamic_slice_in_dim(sum4, (1 - hi) * half, half, 0).astype(F16)
    far = _flip(_after(out, p1, p3), "zl", 2)
    sum8 = (lax.dynamic_slice_in_dim(sum4, hi * half, half, 0) + far.astype(F32)).astype(F16)
    peer = _flip(sum8, "zl", 2)
    mine = jnp.where(hi == 0, jnp.concatenate([sum8, peer]), jnp.concatenate([peer, sum8]))

    def grad(half, own, *far):
        return _call(
            functools.partial(_grad_kernel, half),
            f"grad{half}",
            [((ROWS, KV), F32)] + [((ROWS, KV), BF)] * 3,
            [pltpu.VMEM((WIDE, KV), F32)],
            in_specs=_vmem(6 + len(far)),
            out_specs=_vmem(4),
        )(own, cotangent, r1, c1, r3, c3, *far)

    def near_keys(own):
        return _call(
            _near_keys_kernel,
            "near_keys",
            [((TOK, KV), F32)] + [((TOK, KV), BF)] * 2,
            [pltpu.VMEM((2 * WIDE, KV), BF)],
            in_specs=_vmem(7),
            out_specs=_vmem(3),
        )(own, r1, r3, *pairs)

    g = grad(0, _after(own, p2), r2)
    a1, a3 = _shift(g[1], "x", 1), _shift(g[3], "x", 3)
    k0, k1, k3 = near_keys(_after(own, g[0], peer))
    e1, e3 = _shift(k1, "y", 3), _shift(k3, "y", 1)
    a2 = _shift(g[2], "x", 2)
    b = grad(1, _after(own, a1, a3), r2, r4)
    (k2,) = _call(
        _far_keys_kernel,
        "far_keys",
        [((TOK, KV), BF)],
        [pltpu.VMEM((2 * WIDE, KV), BF)],
        in_specs=_vmem(6),
        out_specs=_vmem(1),
    )(r2, _after(r4, k0), *pairs)
    next_layer = _flip(_after(mine, g[0]), "zl", 1)
    swapped = [_shift(_after(v, a1, a3), "core", 1, 2) for v in (mine, next_layer)]
    far_sum = (_after(g[0], b[0]) + sum(v.astype(F32) for v in (a1, a2, a3))).astype(BF)
    from_zh = _shift(far_sum, "zh", 1, 2)
    b1, b3 = [_shift(_after(b[k], a1, a3), "x", k) for k in (1, 3)]
    b2 = _shift(_after(b[2], far_sum, swapped[1]), "x", 2)
    weight_grad = (b[0] + sum(v.astype(F32) for v in (b1, b3, b2, from_zh)))[None]

    e2 = _shift(_after(k2, e1, e3), "y", 2)
    keys = k0 + sum(v.astype(F32) for v in (e1, e3, e2))

    averages = [mine, next_layer] + swapped
    averages = [v.astype(F32) / (8.0 * UNIT) for v in averages]

    def layer_of(k, place):
        return (jnp.where(k < 2, place[0], 1 - place[0]) * 2 + (place[1] ^ (k & 1)), 0, 0)

    block = pl.BlockSpec((1, ROWS, KV), layer_of)
    whole = pl.BlockSpec((ROWS, KV), lambda k, place: (0, 0))
    new_global, new_momentum = pl.pallas_call(
        _outer_kernel,
        name="outer_step",
        out_shape=[jax.ShapeDtypeStruct((4, ROWS, KV), F32)] * 2,
        grid_spec=pltpu.PrefetchScalarGridSpec(
            num_scalar_prefetch=1,
            grid=(4,),
            in_specs=[whole] * 4 + [block, block],
            out_specs=[block, block],
        ),
        compiler_params=pltpu.CompilerParams(vmem_limit_bytes=LIMIT),
        cost_estimate=pl.CostEstimate(flops=0, bytes_accessed=1024, transcendentals=0),
    )(jnp.stack([core, lo]).astype(jnp.int32), *averages, global_fragment, momentum)
    return keys.astype(BF), weight_grad, new_global, new_momentum


def solution(mesh):
    split = Mesh(mesh.devices.reshape(4, 2, 2, 4, 4), ("zl", "core", "zh", "y", "x"))
    replica, fsdp = ("zl", "core"), ("zh", "y", "x")
    placed = (
        P(replica),
        P(replica + fsdp, None),
        P(),
        P(replica + fsdp, None),
        P(replica, None, fsdp, None),
        P(None, fsdp, None),
        P(None, fsdp, None),
    )
    return jax.shard_map(
        body,
        mesh=split,
        in_specs=placed,
        out_specs=(
            P(replica + fsdp, None),
            P(replica, fsdp, None),
            P(None, fsdp, None),
            P(None, fsdp, None),
        ),
        check_vma=False,
    )
```

```python
import functools

import jax
import jax.numpy as jnp
from jax import lax
from jax.experimental import pallas as pl
from jax.experimental.pallas import tpu as pltpu
from jax.sharding import Mesh, PartitionSpec as P

D = 4608
KV = 1024
ROWS = 144
WIDE = 576
TOK = 256
MSG = 2 * WIDE + KV
SCALE = float(D) ** -0.5
BF = jnp.bfloat16
F32 = jnp.float32
F16 = jnp.float16
UNIT = 512.0
LIMIT = 48 * 1024 * 1024


def _place():
    return [lax.axis_index(n) for n in ("zl", "core", "zh", "y", "x")]


def _shift(v, axis, k, size=4):
    return lax.ppermute(v, axis, [(i, (i + k) % size) for i in range(size)])


def _flip(v, axis, bit, size=4):
    return lax.ppermute(v, axis, [(i, i ^ bit) for i in range(size)])


def _after(v, *done):
    return lax.optimization_barrier((v, *done))[0]


def _call(kernel, name, outs, scratch=(), **kw):
    return pl.pallas_call(
        kernel,
        name=name,
        out_shape=[jax.ShapeDtypeStruct(s, d) for s, d in outs],
        scratch_shapes=list(scratch),
        compiler_params=pltpu.CompilerParams(vmem_limit_bytes=LIMIT),
        cost_estimate=pl.CostEstimate(flops=0, bytes_accessed=1024, transcendentals=0),
        **kw,
    )


def _vmem(n):
    return [pl.BlockSpec(memory_space=pltpu.VMEM)] * n


def _pick_kernel(index_ref, frag_ref, used_ref, give_ref, keep_ref, sems):
    core = _place()[1]
    copies = [
        pltpu.make_async_copy(frag_ref.at[0, index_ref[0]], used_ref, sems.at[0]),
        pltpu.make_async_copy(frag_ref.at[0, pl.ds(2 - 2 * core, 2)], give_ref, sems.at[1]),
        pltpu.make_async_copy(frag_ref.at[0, pl.ds(2 * core, 2)], keep_ref, sems.at[2]),
    ]
    for c in copies:
        c.start()
    for c in copies:
        c.wait()


def _norm_kernel(x_ref, gain_ref, cot_ref, own_ref, n1_ref, m2_ref, n3_ref, held):
    _, _, zh, y, _ = _place()
    values = x_ref[...].astype(F32)
    stats = jnp.mean(values * values, axis=1, keepdims=True)
    normed = (values * lax.rsqrt(stats + 1e-06) * gain_ref[...]).astype(BF)
    for q in range(8):
        held[q] = normed[:, q * WIDE : (q + 1) * WIDE]
    for k, out in enumerate((own_ref, n1_ref, m2_ref, n3_ref)):
        chunk = (y + k) & 3
        out[:, : 2 * WIDE] = jnp.concatenate([held[(1 - zh) * 4 + chunk], held[zh * 4 + chunk]], axis=1)
    m2_ref[:, 2 * WIDE :] = cot_ref[...]


def _grad_kernel(half, n0, c0, n1, c1, m2, n3, c3, own_ref, o1_ref, o2_ref, o3_ref, total):
    x = _place()[4]
    first = half * WIDE
    normed = jnp.concatenate([n[:, first : first + WIDE] for n in (n0, n1, m2, n3)], axis=0)
    cot = jnp.concatenate([c0[...], c1[...], m2[:, 2 * WIDE :], c3[...]], axis=0)
    total[...] = lax.dot_general(normed, cot, (((0,), (0,)), ((), ())), preferred_element_type=F32)
    for k, out in enumerate((own_ref, o1_ref, o2_ref, o3_ref)):
        rows = pl.ds(pl.multiple_of(((x + k) & 3) * ROWS, 16), ROWS)
        out[...] = (total[rows, :] * SCALE).astype(out.dtype)


def _keys_kernel(n, *refs):
    blocks, pairs, outs, layer = refs[:n], refs[n : n + 4], refs[n + 4 : 2 * n + 4], refs[-1]
    x = _place()[4]
    for k in range(4):
        for h in range(2):
            first = pl.multiple_of(h * WIDE + ((x + 4 - k) & 3) * ROWS, 16)
            layer[pl.ds(first, ROWS), :] = pairs[k][h]
    for block, out in zip(blocks, outs):
        part = jnp.dot(block[:, : 2 * WIDE], layer[...], preferred_element_type=F32)
        out[...] = (part * SCALE).astype(out.dtype)


def _outer_kernel(place_ref, *refs):
    averages, (global_ref, momentum_ref, new_global_ref, new_momentum_ref) = refs[:4], refs[4:]

    for k in range(4):

        @pl.when(pl.program_id(0) == k)
        def _():
            mean = averages[k][...]
            momentum = 0.9 * momentum_ref[0] + mean
            new_momentum_ref[0] = momentum
            new_global_ref[0] = global_ref[0] - 0.7 * (mean + 0.9 * momentum)


def body(layer_index, inputs, norm_gain, cotangent, local_fragment, global_fragment, momentum):
    zl, core = lax.axis_index("zl"), lax.axis_index("core")
    hi, lo = zl >> 1, zl & 1
    any_spec = pl.BlockSpec(memory_space=pl.ANY)

    used, give, keep = _call(
        _pick_kernel,
        "pick",
        [((ROWS, KV), BF)] + [((2, ROWS, KV), BF)] * 2,
        [pltpu.SemaphoreType.DMA((3,))],
        in_specs=[pl.BlockSpec(memory_space=pltpu.SMEM), any_spec],
        out_specs=[any_spec] * 3,
    )(layer_index, local_fragment)
    c1, c3 = _shift(cotangent, "y", 1), _shift(cotangent, "y", 3)
    used_other = _shift(used, "zh", 1, 2)
    got = _shift(give, "core", 1, 2)

    rows = 64
    tile = lambda n: pl.BlockSpec((rows, n), lambda i: (i, 0))
    own, n1, m2, n3 = _call(
        _norm_kernel,
        "normed",
        [((TOK, n), BF) for n in (2 * WIDE, 2 * WIDE, MSG, 2 * WIDE)],
        [pltpu.VMEM((8, rows, WIDE), BF)],
        grid=(TOK // rows,),
        in_specs=[tile(D), pl.BlockSpec((1, D), lambda i: (0, 0)), tile(KV)],
        out_specs=[tile(n) for n in (2 * WIDE, 2 * WIDE, MSG, 2 * WIDE)],
    )(inputs, _after(norm_gain[None, :], used), cotangent)

    pair = jnp.stack([_after(used_other, c1, c3), used])
    p1, p3 = _shift(pair, "x", 1), _shift(pair, "x", 3)
    r1, r3 = _shift(_after(n1, c1, c3), "y", 1), _shift(_after(n3, c1, c3), "y", 3)

    got = _after(got, own, used_other)

    def delta(which):
        shared = lax.dynamic_index_in_dim(global_fragment, 2 * core + which, 0, keepdims=False)
        first = lax.dynamic_index_in_dim(keep, which, 0, keepdims=False).astype(F32)
        second = lax.dynamic_index_in_dim(got, which, 0, keepdims=False).astype(F32)
        return ((shared - first) + (shared - second)) * UNIT

    half = ROWS // 2
    sum4 = delta(lo) + _after(_flip(delta(1 - lo).astype(F16), "zl", 1), r1, r3, p1, p3).astype(F32)
    out = lax.dynamic_slice_in_dim(sum4, (1 - hi) * half, half, 0).astype(F16)
    other = _flip(out, "zl", 2)
    sum8 = (lax.dynamic_slice_in_dim(sum4, hi * half, half, 0) + other.astype(F32)).astype(F16)
    peer = _flip(sum8, "zl", 2)
    mine = jnp.where(hi == 0, jnp.concatenate([sum8, peer]), jnp.concatenate([peer, sum8]))
    next_layer = _flip(mine, "zl", 1)

    r2 = _shift(_after(m2, r1, r3, pair), "y", 2)
    pairs = [pair, p1, _shift(_after(pair, p1, p3), "x", 2), p3]

    def keys_of(*blocks):
        return _call(
            functools.partial(_keys_kernel, len(blocks)),
            f"keys{len(blocks)}",
            [((TOK, KV), F32 if b is own else BF) for b in blocks],
            [pltpu.VMEM((2 * WIDE, KV), BF)],
            in_specs=_vmem(len(blocks) + 4),
            out_specs=_vmem(len(blocks)),
        )(*blocks, *pairs)

    k0, k1, k3 = keys_of(own, r1, r3)
    e1, e3 = _shift(k1, "y", 3), _shift(k3, "y", 1)

    def grad(half, own):
        return _call(
            functools.partial(_grad_kernel, half),
            f"grad{half}",
            [((ROWS, KV), F32)] + [((ROWS, KV), BF)] * 3,
            [pltpu.VMEM((WIDE, KV), F32)],
            in_specs=_vmem(7),
            out_specs=_vmem(4),
        )(own, cotangent, r1, c1, r2, r3, c3)

    g = grad(0, _after(own, k0))
    a1, a3 = _shift(g[1], "x", 1), _shift(g[3], "x", 3)
    b = grad(1, own)
    a2 = _shift(_after(g[2], a1), "x", 2)
    (k2,) = keys_of(_after(r2, b[0], e1, e3, a1, a3))
    swapped = [_shift(_after(v, a1, a3), "core", 1, 2) for v in (mine, next_layer)]
    far_sum = (g[0] + sum(v.astype(F32) for v in (a1, a2, a3))).astype(BF)
    from_zh = _shift(far_sum, "zh", 1, 2)
    b1, b3, b2 = [_shift(_after(b[k], far_sum), "x", k) for k in (1, 3, 2)]
    weight_grad = (b[0] + sum(v.astype(F32) for v in (b1, b3, b2, from_zh)))[None]

    averages = [mine, next_layer] + swapped
    averages = [v.astype(F32) / (8.0 * UNIT) for v in averages]

    def layer_of(k, place):
        return (jnp.where(k < 2, place[0], 1 - place[0]) * 2 + (place[1] ^ (k & 1)), 0, 0)

    block = pl.BlockSpec((1, ROWS, KV), layer_of)
    whole = pl.BlockSpec((ROWS, KV), lambda k, place: (0, 0))
    new_global, new_momentum = pl.pallas_call(
        _outer_kernel,
        name="outer_step",
        out_shape=[jax.ShapeDtypeStruct((4, ROWS, KV), F32)] * 2,
        grid_spec=pltpu.PrefetchScalarGridSpec(
            num_scalar_prefetch=1,
            grid=(4,),
            in_specs=[whole] * 4 + [block, block],
            out_specs=[block, block],
        ),
        compiler_params=pltpu.CompilerParams(vmem_limit_bytes=LIMIT),
        cost_estimate=pl.CostEstimate(flops=0, bytes_accessed=1024, transcendentals=0),
    )(jnp.stack([core, lo]).astype(jnp.int32), *averages, global_fragment, momentum)

    e2 = _shift(_after(k2, b[0]), "y", 2)
    keys = k0 + sum(v.astype(F32) for v in (e1, e3, e2))
    return keys.astype(BF), weight_grad, new_global, new_momentum


def solution(mesh):
    split = Mesh(mesh.devices.reshape(4, 2, 2, 4, 4), ("zl", "core", "zh", "y", "x"))
    replica, fsdp = ("zl", "core"), ("zh", "y", "x")
    placed = (
        P(replica),
        P(replica + fsdp, None),
        P(),
        P(replica + fsdp, None),
        P(replica, None, fsdp, None),
        P(None, fsdp, None),
        P(None, fsdp, None),
    )
    return jax.shard_map(
        body,
        mesh=split,
        in_specs=placed,
        out_specs=(
            P(replica + fsdp, None),
            P(replica, fsdp, None),
            P(None, fsdp, None),
            P(None, fsdp, None),
        ),
        check_vma=False,
    )
```

```python
import functools

import jax
import jax.numpy as jnp
from jax import lax
from jax.experimental import pallas as pl
from jax.experimental.pallas import tpu as pltpu
from jax.sharding import Mesh, PartitionSpec as P

D = 4608
KV = 1024
ROWS = 144
WIDE = 576
TOK = 256
MSG = 2 * WIDE + KV
SCALE = float(D) ** -0.5
BF = jnp.bfloat16
F32 = jnp.float32
F16 = jnp.float16
UNIT = 512.0
LIMIT = 48 * 1024 * 1024


def _place():
    return [lax.axis_index(n) for n in ("zl", "core", "zh", "y", "x")]


def _shift(v, axis, k, size=4):
    return lax.ppermute(v, axis, [(i, (i + k) % size) for i in range(size)])


def _flip(v, axis, bit, size=4):
    return lax.ppermute(v, axis, [(i, i ^ bit) for i in range(size)])


def _after(v, *done):
    return lax.optimization_barrier((v, *done))[0]


def _call(kernel, name, outs, scratch=(), **kw):
    return pl.pallas_call(
        kernel,
        name=name,
        out_shape=[jax.ShapeDtypeStruct(s, d) for s, d in outs],
        scratch_shapes=list(scratch),
        compiler_params=pltpu.CompilerParams(vmem_limit_bytes=LIMIT),
        cost_estimate=pl.CostEstimate(flops=0, bytes_accessed=1024, transcendentals=0),
        **kw,
    )


def _vmem(n):
    return [pl.BlockSpec(memory_space=pltpu.VMEM)] * n


def _pick_kernel(index_ref, frag_ref, used_ref, give_ref, keep_ref, sems):
    core = _place()[1]
    copies = [
        pltpu.make_async_copy(frag_ref.at[0, index_ref[0]], used_ref, sems.at[0]),
        pltpu.make_async_copy(frag_ref.at[0, pl.ds(2 - 2 * core, 2)], give_ref, sems.at[1]),
        pltpu.make_async_copy(frag_ref.at[0, pl.ds(2 * core, 2)], keep_ref, sems.at[2]),
    ]
    for c in copies:
        c.start()
    for c in copies:
        c.wait()


def _norm_kernel(x_ref, gain_ref, cot_ref, own_ref, n1_ref, m2_ref, n3_ref, held):
    _, _, zh, y, _ = _place()
    values = x_ref[...].astype(F32)
    stats = jnp.mean(values * values, axis=1, keepdims=True)
    normed = (values * lax.rsqrt(stats + 1e-06) * gain_ref[...]).astype(BF)
    for q in range(8):
        held[q] = normed[:, q * WIDE : (q + 1) * WIDE]
    for k, out in enumerate((own_ref, n1_ref, m2_ref, n3_ref)):
        chunk = (y + k) & 3
        out[:, : 2 * WIDE] = jnp.concatenate([held[(1 - zh) * 4 + chunk], held[zh * 4 + chunk]], axis=1)
    m2_ref[:, 2 * WIDE :] = cot_ref[...]


def _grad_kernel(half, n0, c0, n1, c1, m2, n3, c3, own_ref, o1_ref, o2_ref, o3_ref, total):
    x = _place()[4]
    first = half * WIDE
    normed = jnp.concatenate([n[:, first : first + WIDE] for n in (n0, n1, m2, n3)], axis=0)
    cot = jnp.concatenate([c0[...], c1[...], m2[:, 2 * WIDE :], c3[...]], axis=0)
    total[...] = lax.dot_general(normed, cot, (((0,), (0,)), ((), ())), preferred_element_type=F32)
    for k, out in enumerate((own_ref, o1_ref, o2_ref, o3_ref)):
        rows = pl.ds(pl.multiple_of(((x + k) & 3) * ROWS, 16), ROWS)
        out[...] = (total[rows, :] * SCALE).astype(out.dtype)


def _keys_kernel(n, *refs):
    blocks, pairs, outs, layer = refs[:n], refs[n : n + 4], refs[n + 4 : 2 * n + 4], refs[-1]
    x = _place()[4]
    for k in range(4):
        for h in range(2):
            first = pl.multiple_of(h * WIDE + ((x + 4 - k) & 3) * ROWS, 16)
            layer[pl.ds(first, ROWS), :] = pairs[k][h]
    for block, out in zip(blocks, outs):
        part = jnp.dot(block[:, : 2 * WIDE], layer[...], preferred_element_type=F32)
        out[...] = (part * SCALE).astype(out.dtype)


def _outer_kernel(place_ref, *refs):
    averages, (global_ref, momentum_ref, new_global_ref, new_momentum_ref) = refs[:4], refs[4:]

    for k in range(4):

        @pl.when(pl.program_id(0) == k)
        def _():
            mean = averages[k][...]
            momentum = 0.9 * momentum_ref[0] + mean
            new_momentum_ref[0] = momentum
            new_global_ref[0] = global_ref[0] - 0.7 * (mean + 0.9 * momentum)


def body(layer_index, inputs, norm_gain, cotangent, local_fragment, global_fragment, momentum):
    zl, core = lax.axis_index("zl"), lax.axis_index("core")
    hi, lo = zl >> 1, zl & 1
    any_spec = pl.BlockSpec(memory_space=pl.ANY)

    used, give, keep = _call(
        _pick_kernel,
        "pick",
        [((ROWS, KV), BF)] + [((2, ROWS, KV), BF)] * 2,
        [pltpu.SemaphoreType.DMA((3,))],
        in_specs=[pl.BlockSpec(memory_space=pltpu.SMEM), any_spec],
        out_specs=[any_spec] * 3,
    )(layer_index, local_fragment)
    c1, c3 = _shift(cotangent, "y", 1), _shift(cotangent, "y", 3)
    used_other = _shift(used, "zh", 1, 2)
    got = _shift(give, "core", 1, 2)

    rows = 64
    tile = lambda n: pl.BlockSpec((rows, n), lambda i: (i, 0))
    own, n1, m2, n3 = _call(
        _norm_kernel,
        "normed",
        [((TOK, n), BF) for n in (2 * WIDE, 2 * WIDE, MSG, 2 * WIDE)],
        [pltpu.VMEM((8, rows, WIDE), BF)],
        grid=(TOK // rows,),
        in_specs=[tile(D), pl.BlockSpec((1, D), lambda i: (0, 0)), tile(KV)],
        out_specs=[tile(n) for n in (2 * WIDE, 2 * WIDE, MSG, 2 * WIDE)],
    )(inputs, _after(norm_gain[None, :], used), cotangent)

    pair = jnp.stack([_after(used_other, c1, c3), used])
    p1, p3 = _shift(pair, "x", 1), _shift(pair, "x", 3)
    r1, r3 = _shift(_after(n1, c1, c3), "y", 1), _shift(_after(n3, c1, c3), "y", 3)

    got = _after(got, own, used_other)

    def delta(which):
        shared = lax.dynamic_index_in_dim(global_fragment, 2 * core + which, 0, keepdims=False)
        first = lax.dynamic_index_in_dim(keep, which, 0, keepdims=False).astype(F32)
        second = lax.dynamic_index_in_dim(got, which, 0, keepdims=False).astype(F32)
        return ((shared - first) + (shared - second)) * UNIT

    half = ROWS // 2
    sum4 = delta(lo) + _after(_flip(delta(1 - lo).astype(F16), "zl", 1), r1, r3, p1, p3).astype(F32)
    out = lax.dynamic_slice_in_dim(sum4, (1 - hi) * half, half, 0).astype(F16)
    other = _flip(out, "zl", 2)
    sum8 = (lax.dynamic_slice_in_dim(sum4, hi * half, half, 0) + other.astype(F32)).astype(F16)
    peer = _flip(sum8, "zl", 2)
    mine = jnp.where(hi == 0, jnp.concatenate([sum8, peer]), jnp.concatenate([peer, sum8]))
    next_layer = _flip(mine, "zl", 1)

    r2 = _shift(_after(m2, r1, r3, pair), "y", 2)
    pairs = [pair, p1, _shift(_after(pair, p1, p3), "x", 2), p3]

    def keys_of(*blocks):
        return _call(
            functools.partial(_keys_kernel, len(blocks)),
            f"keys{len(blocks)}",
            [((TOK, KV), F32 if b is own else BF) for b in blocks],
            [pltpu.VMEM((2 * WIDE, KV), BF)],
            in_specs=_vmem(len(blocks) + 4),
            out_specs=_vmem(len(blocks)),
        )(*blocks, *pairs)

    k0, k1, k3 = keys_of(own, r1, r3)
    e1, e3 = _shift(k1, "y", 3), _shift(k3, "y", 1)

    def grad(half, own):
        return _call(
            functools.partial(_grad_kernel, half),
            f"grad{half}",
            [((ROWS, KV), F32)] + [((ROWS, KV), BF)] * 3,
            [pltpu.VMEM((WIDE, KV), F32)],
            in_specs=_vmem(7),
            out_specs=_vmem(4),
        )(own, cotangent, r1, c1, r2, r3, c3)

    g = grad(0, _after(own, k0))
    a1, a3 = _shift(g[1], "x", 1), _shift(g[3], "x", 3)
    b = grad(1, own)
    a2 = _shift(_after(g[2], a1), "x", 2)
    (k2,) = keys_of(_after(r2, b[0], a1, a3))
    swapped = [_shift(_after(v, a1, a3), "core", 1, 2) for v in (mine, next_layer)]
    far_sum = (g[0] + sum(v.astype(F32) for v in (a1, a2, a3))).astype(BF)
    from_zh = _shift(far_sum, "zh", 1, 2)
    b1, b3, b2 = [_shift(_after(b[k], far_sum), "x", k) for k in (1, 3, 2)]
    weight_grad = (b[0] + sum(v.astype(F32) for v in (b1, b3, b2, from_zh)))[None]

    averages = [mine, next_layer] + swapped
    averages = [v.astype(F32) / (8.0 * UNIT) for v in averages]

    def layer_of(k, place):
        return (jnp.where(k < 2, place[0], 1 - place[0]) * 2 + (place[1] ^ (k & 1)), 0, 0)

    block = pl.BlockSpec((1, ROWS, KV), layer_of)
    whole = pl.BlockSpec((ROWS, KV), lambda k, place: (0, 0))
    new_global, new_momentum = pl.pallas_call(
        _outer_kernel,
        name="outer_step",
        out_shape=[jax.ShapeDtypeStruct((4, ROWS, KV), F32)] * 2,
        grid_spec=pltpu.PrefetchScalarGridSpec(
            num_scalar_prefetch=1,
            grid=(4,),
            in_specs=[whole] * 4 + [block, block],
            out_specs=[block, block],
        ),
        compiler_params=pltpu.CompilerParams(vmem_limit_bytes=LIMIT),
        cost_estimate=pl.CostEstimate(flops=0, bytes_accessed=1024, transcendentals=0),
    )(jnp.stack([core, lo]).astype(jnp.int32), *averages, global_fragment, momentum)

    e2 = _shift(_after(k2, b[0], e1, e3), "y", 2)
    keys = k0 + sum(v.astype(F32) for v in (e1, e3, e2))
    return keys.astype(BF), weight_grad, new_global, new_momentum


def solution(mesh):
    split = Mesh(mesh.devices.reshape(4, 2, 2, 4, 4), ("zl", "core", "zh", "y", "x"))
    replica, fsdp = ("zl", "core"), ("zh", "y", "x")
    placed = (
        P(replica),
        P(replica + fsdp, None),
        P(),
        P(replica + fsdp, None),
        P(replica, None, fsdp, None),
        P(None, fsdp, None),
        P(None, fsdp, None),
    )
    return jax.shard_map(
        body,
        mesh=split,
        in_specs=placed,
        out_specs=(
            P(replica + fsdp, None),
            P(replica, fsdp, None),
            P(None, fsdp, None),
            P(None, fsdp, None),
        ),
        check_vma=False,
    )
```

```python
import functools

import jax
import jax.numpy as jnp
from jax import lax
from jax.experimental import pallas as pl
from jax.experimental.pallas import tpu as pltpu
from jax.sharding import Mesh, PartitionSpec as P

D = 4608
KV = 1024
ROWS = 144
WIDE = 576
TOK = 256
MSG = 2 * WIDE + KV
SCALE = float(D) ** -0.5
BF = jnp.bfloat16
F32 = jnp.float32
F16 = jnp.float16
UNIT = 512.0
LIMIT = 48 * 1024 * 1024


def _place():
    return [lax.axis_index(n) for n in ("zl", "core", "zh", "y", "x")]


def _shift(v, axis, k, size=4):
    return lax.ppermute(v, axis, [(i, (i + k) % size) for i in range(size)])


def _flip(v, axis, bit, size=4):
    return lax.ppermute(v, axis, [(i, i ^ bit) for i in range(size)])


def _after(v, *done):
    return lax.optimization_barrier((v, *done))[0]


def _call(kernel, name, outs, scratch=(), **kw):
    return pl.pallas_call(
        kernel,
        name=name,
        out_shape=[jax.ShapeDtypeStruct(s, d) for s, d in outs],
        scratch_shapes=list(scratch),
        compiler_params=pltpu.CompilerParams(vmem_limit_bytes=LIMIT),
        cost_estimate=pl.CostEstimate(flops=0, bytes_accessed=1024, transcendentals=0),
        **kw,
    )


def _vmem(n):
    return [pl.BlockSpec(memory_space=pltpu.VMEM)] * n


def _pick_kernel(index_ref, frag_ref, used_ref, give_ref, keep_ref, sems):
    core = _place()[1]
    copies = [
        pltpu.make_async_copy(frag_ref.at[0, index_ref[0]], used_ref, sems.at[0]),
        pltpu.make_async_copy(frag_ref.at[0, pl.ds(2 - 2 * core, 2)], give_ref, sems.at[1]),
        pltpu.make_async_copy(frag_ref.at[0, pl.ds(2 * core, 2)], keep_ref, sems.at[2]),
    ]
    for c in copies:
        c.start()
    for c in copies:
        c.wait()


def _norm_kernel(x_ref, gain_ref, cot_ref, own_ref, n1_ref, m2_ref, n3_ref, held):
    _, _, zh, y, _ = _place()
    values = x_ref[...].astype(F32)
    stats = jnp.mean(values * values, axis=1, keepdims=True)
    normed = (values * lax.rsqrt(stats + 1e-06) * gain_ref[...][None, :]).astype(BF)
    for q in range(8):
        held[q] = normed[:, q * WIDE : (q + 1) * WIDE]
    for k, out in enumerate((own_ref, n1_ref, m2_ref, n3_ref)):
        chunk = (y + k) & 3
        out[:, : 2 * WIDE] = jnp.concatenate([held[(1 - zh) * 4 + chunk], held[zh * 4 + chunk]], axis=1)
    m2_ref[:, 2 * WIDE :] = cot_ref[...]


def _grad_kernel(half, n0, c0, n1, c1, m2, n3, c3, own_ref, o1_ref, o2_ref, o3_ref, total):
    x = _place()[4]
    first = half * WIDE
    normed = jnp.concatenate([n[:, first : first + WIDE] for n in (n0, n1, m2, n3)], axis=0)
    cot = jnp.concatenate([c0[...], c1[...], m2[:, 2 * WIDE :], c3[...]], axis=0)
    total[...] = lax.dot_general(normed, cot, (((0,), (0,)), ((), ())), preferred_element_type=F32)
    for k, out in enumerate((own_ref, o1_ref, o2_ref, o3_ref)):
        rows = pl.ds(pl.multiple_of(((x + k) & 3) * ROWS, 16), ROWS)
        out[...] = (total[rows, :] * SCALE).astype(out.dtype)


def _keys_kernel(n, *refs):
    blocks, pairs, outs, layer = refs[:n], refs[n : n + 4], refs[n + 4 : 2 * n + 4], refs[-1]
    x = _place()[4]
    for k in range(4):
        for h in range(2):
            first = pl.multiple_of(h * WIDE + ((x + 4 - k) & 3) * ROWS, 16)
            layer[pl.ds(first, ROWS), :] = pairs[k][h]
    for block, out in zip(blocks, outs):
        part = jnp.dot(block[:, : 2 * WIDE], layer[...], preferred_element_type=F32)
        out[...] = (part * SCALE).astype(out.dtype)


def _outer_kernel(place_ref, *refs):
    averages, (global_ref, momentum_ref, new_global_ref, new_momentum_ref) = refs[:4], refs[4:]

    for k in range(4):

        @pl.when(pl.program_id(0) == k)
        def _():
            mean = averages[k][...]
            momentum = 0.9 * momentum_ref[0] + mean
            new_momentum_ref[0] = momentum
            new_global_ref[0] = global_ref[0] - 0.7 * (mean + 0.9 * momentum)


def body(layer_index, inputs, norm_gain, cotangent, local_fragment, global_fragment, momentum):
    zl, core = lax.axis_index("zl"), lax.axis_index("core")
    hi, lo = zl >> 1, zl & 1
    any_spec = pl.BlockSpec(memory_space=pl.ANY)

    used, give, keep = _call(
        _pick_kernel,
        "pick",
        [((ROWS, KV), BF)] + [((2, ROWS, KV), BF)] * 2,
        [pltpu.SemaphoreType.DMA((3,))],
        in_specs=[pl.BlockSpec(memory_space=pltpu.SMEM), any_spec],
        out_specs=[any_spec] * 3,
    )(layer_index, local_fragment)
    c1, c3 = _shift(cotangent, "y", 1), _shift(cotangent, "y", 3)
    used_other = _shift(used, "zh", 1, 2)
    got = _shift(give, "core", 1, 2)

    rows = 64
    tile = lambda n: pl.BlockSpec((rows, n), lambda i: (i, 0))
    own, n1, m2, n3 = _call(
        _norm_kernel,
        "normed",
        [((TOK, n), BF) for n in (2 * WIDE, 2 * WIDE, MSG, 2 * WIDE)],
        [pltpu.VMEM((8, rows, WIDE), BF)],
        grid=(TOK // rows,),
        in_specs=[tile(D), pl.BlockSpec((D,), lambda i: (0,)), tile(KV)],
        out_specs=[tile(n) for n in (2 * WIDE, 2 * WIDE, MSG, 2 * WIDE)],
    )(inputs, _after(norm_gain, used), cotangent)

    pair = jnp.stack([_after(used_other, c1, c3), used])
    p1, p3 = _shift(pair, "x", 1), _shift(pair, "x", 3)
    r1, r3 = _shift(_after(n1, c1, c3), "y", 1), _shift(_after(n3, c1, c3), "y", 3)

    got = _after(got, own, used_other)

    def delta(which):
        shared = lax.dynamic_index_in_dim(global_fragment, 2 * core + which, 0, keepdims=False)
        first = lax.dynamic_index_in_dim(keep, which, 0, keepdims=False).astype(F32)
        second = lax.dynamic_index_in_dim(got, which, 0, keepdims=False).astype(F32)
        return ((shared - first) + (shared - second)) * UNIT

    half = ROWS // 2
    sum4 = delta(lo) + _after(_flip(delta(1 - lo).astype(F16), "zl", 1), r1, r3, p1, p3).astype(F32)
    out = lax.dynamic_slice_in_dim(sum4, (1 - hi) * half, half, 0).astype(F16)
    other = _flip(out, "zl", 2)
    sum8 = (lax.dynamic_slice_in_dim(sum4, hi * half, half, 0) + other.astype(F32)).astype(F16)
    peer = _flip(sum8, "zl", 2)
    mine = jnp.where(hi == 0, jnp.concatenate([sum8, peer]), jnp.concatenate([peer, sum8]))
    next_layer = _flip(mine, "zl", 1)

    r2 = _shift(_after(m2, r1, r3, pair), "y", 2)
    pairs = [pair, p1, _shift(_after(pair, p1, p3), "x", 2), p3]

    def keys_of(*blocks):
        return _call(
            functools.partial(_keys_kernel, len(blocks)),
            f"keys{len(blocks)}",
            [((TOK, KV), F32 if b is own else BF) for b in blocks],
            [pltpu.VMEM((2 * WIDE, KV), BF)],
            in_specs=_vmem(len(blocks) + 4),
            out_specs=_vmem(len(blocks)),
        )(*blocks, *pairs)

    k0, k1, k3 = keys_of(own, r1, r3)
    e1, e3 = _shift(k1, "y", 3), _shift(k3, "y", 1)

    def grad(half, own):
        return _call(
            functools.partial(_grad_kernel, half),
            f"grad{half}",
            [((ROWS, KV), F32)] + [((ROWS, KV), BF)] * 3,
            [pltpu.VMEM((WIDE, KV), F32)],
            in_specs=_vmem(7),
            out_specs=_vmem(4),
        )(own, cotangent, r1, c1, r2, r3, c3)

    g = grad(0, _after(own, k0))
    a1, a3 = _shift(g[1], "x", 1), _shift(g[3], "x", 3)
    b = grad(1, own)
    a2 = _shift(_after(g[2], a1), "x", 2)
    (k2,) = keys_of(_after(r2, b[0], a1, a3))
    swapped = [_shift(_after(v, a1, a3), "core", 1, 2) for v in (mine, next_layer)]
    far_sum = (g[0] + sum(v.astype(F32) for v in (a1, a2, a3))).astype(BF)
    from_zh = _shift(far_sum, "zh", 1, 2)
    b1, b3, b2 = [_shift(_after(b[k], far_sum), "x", k) for k in (1, 3, 2)]
    weight_grad = (b[0] + sum(v.astype(F32) for v in (b1, b3, b2, from_zh)))[None]

    averages = [mine, next_layer] + swapped
    averages = [v.astype(F32) / (8.0 * UNIT) for v in averages]

    def layer_of(k, place):
        return (jnp.where(k < 2, place[0], 1 - place[0]) * 2 + (place[1] ^ (k & 1)), 0, 0)

    block = pl.BlockSpec((1, ROWS, KV), layer_of)
    whole = pl.BlockSpec((ROWS, KV), lambda k, place: (0, 0))
    new_global, new_momentum = pl.pallas_call(
        _outer_kernel,
        name="outer_step",
        out_shape=[jax.ShapeDtypeStruct((4, ROWS, KV), F32)] * 2,
        grid_spec=pltpu.PrefetchScalarGridSpec(
            num_scalar_prefetch=1,
            grid=(4,),
            in_specs=[whole] * 4 + [block, block],
            out_specs=[block, block],
        ),
        compiler_params=pltpu.CompilerParams(vmem_limit_bytes=LIMIT),
        cost_estimate=pl.CostEstimate(flops=0, bytes_accessed=1024, transcendentals=0),
    )(jnp.stack([core, lo]).astype(jnp.int32), *averages, global_fragment, momentum)

    e2 = _shift(_after(k2, b[0], e1, e3), "y", 2)
    keys = k0 + sum(v.astype(F32) for v in (e1, e3, e2))
    return keys.astype(BF), weight_grad, new_global, new_momentum


def solution(mesh):
    split = Mesh(mesh.devices.reshape(4, 2, 2, 4, 4), ("zl", "core", "zh", "y", "x"))
    replica, fsdp = ("zl", "core"), ("zh", "y", "x")
    placed = (
        P(replica),
        P(replica + fsdp, None),
        P(),
        P(replica + fsdp, None),
        P(replica, None, fsdp, None),
        P(None, fsdp, None),
        P(None, fsdp, None),
    )
    return jax.shard_map(
        body,
        mesh=split,
        in_specs=placed,
        out_specs=(
            P(replica + fsdp, None),
            P(replica, fsdp, None),
            P(None, fsdp, None),
            P(None, fsdp, None),
        ),
        check_vma=False,
    )
```
